512 devices in a mesh: rep: 32 (over z_hi, x, core), grp: 16 (over y, z_lo).
Axes of the slice: x: 4, y: 4, z: 16 (z_hi: 4, z_lo: 4; z = z_hi * 4 + z_lo), core: 2. Of those that a mesh axis runs over, the one named last changes fastest.
Arguments:
- tokens: bfloat16 [98304, 2048], P(('rep', 'grp')), may hold values from -24 to 24
- norm_gain: float32 [2048], replicated, may hold values from 0.5 to 1.5
- weight_codes: int32 [2048, 512], P('grp'), may hold values from -127 to 127
- block_scales: float32 [16, 512], P('grp'), may hold values from 0.00013258251 to 0.00053033006
- key_grad: bfloat16 [98304, 512], P(('rep', 'grp')), may hold values from -6 to 6
Outputs:
- keys: bfloat16 [98304, 512], P(('rep', 'grp'))
- tokens_grad: bfloat16 [98304, 2048], P(('rep', 'grp'))
- weight_grad: float32 [2048, 512], P('grp')
- gain_grad: float32 [2048], replicated
The draws below stay inside these ranges and needn't reach their ends.
Inputs may be any that keep to these rules, and one draw needn't show every extreme that they name: `weight_codes`: signed 8-bit codes.
All inputs are finite; a program needn't handle non-finite values.
Results may differ from the reference program's by a relative error of at most 0.0057.
Values may be sent and summed in bfloat16 or wider, within the bound.
No kernel may reach another device: no remote copies, remote signals or barrier semaphores. Data moves between devices by JAX's collectives and lax.ppermute only.
A program may use at most 64 MiB of HBM per device.

```python
import math
import jax
import jax.numpy as jnp
from jax import lax

D = 2048
KV = 512
BLOCK = 128
TOKENS = 98304
N_REP = 32
N_GRP = 16


def set_ends(drawn, own_key, smallest, high):
    extent = drawn.shape
    spot = [jax.random.randint(jax.random.fold_in(own_key, axis), (), 0, extent[axis]) for axis in range(len(extent))]
    drawn = drawn.at[tuple(spot)].set(smallest)
    longest = extent.index(max(extent))
    spot[longest] = (spot[longest] + 1) % extent[longest]
    return drawn.at[tuple(spot)].set(high)


def with_spikes(entries, stream_key, source, target, shards_of, factor):
    def block_of(position):
        return (jnp.arange(entries.shape[position]) // (entries.shape[position] // shards_of)).reshape((-1,) + (1,) * (entries.ndim - 1 - position))

    first = jax.random.permutation(stream_key, shards_of)[block_of(target)]
    far = (block_of(target) + shards_of // 2) % shards_of
    return jnp.where((block_of(source) == first) | (block_of(source) == far), factor * entries, entries)


def shard_levels(rng, dims, shards, low, largest):
    def one(position, blocks):
        heights = jax.random.uniform(jax.random.fold_in(jax.random.fold_in(rng, 6), position), (blocks,), jnp.float32, low / len(shards), largest / len(shards))
        return jnp.repeat(jnp.exp(heights), dims[position] // blocks).reshape((-1,) + (1,) * (len(dims) - position - 1))

    level = one(*shards[0])
    for cut in shards[1:]:
        level = level * one(*cut)
    return level


def scatter_about(stream_key, shape, deviation, most, pieces=(), dtype=jnp.bfloat16):
    result = deviation * jax.random.normal(stream_key, shape, jnp.float32)
    if pieces:
        result = result * shard_levels(stream_key, shape, pieces, -0.22, 0.18)
    return jnp.clip(result, -most, most).astype(dtype)


def bell_draw_with(rng, shape, deviation, most, split, heavy, kind=jnp.bfloat16):
    result = deviation * jax.random.normal(rng, shape, jnp.float32)
    if split:
        result = result * shard_levels(rng, shape, split, -0.22, 0.18)
    return jnp.clip(with_spikes(result, jax.random.fold_in(rng, 3), *heavy), -most, most).astype(kind)


def setup_inputs(seed: int = 0) -> dict:
    splits = jax.random.split(jax.random.key(seed), 6)
    tokens = bell_draw_with(splits[0], (TOKENS, D), 1.0, 24.0, ((0, 512),), (0, 1, 512, 6.0))
    norm_gain = jnp.clip(1.0 + 0.1 * jax.random.normal(splits[1], (D,), jnp.float32), 0.5, 1.5)
    weight_codes = set_ends(jax.random.randint(splits[2], (D, KV), -127, 128), jax.random.fold_in(splits[2], 1), -127, 127).astype(jnp.int32)
    block_scales = jnp.clip(jnp.exp(math.log(0.00053033006) - 1.3862944 * jax.random.uniform(splits[3], (D // BLOCK, KV), jnp.float32) ** shard_levels(splits[3], (D // BLOCK, KV), ((0, 16),), -0.2, 0.2)), 0.00013258251, 0.00053033006)
    key_grad = scatter_about(splits[4], (TOKENS, KV), 1.0, 6.0, ((0, 512),))
    return {"tokens": tokens, "norm_gain": norm_gain, "weight_codes": weight_codes, "block_scales": block_scales, "key_grad": key_grad}


eps = 1e-05

def reference(tokens, norm_gain, weight_codes, block_scales, key_grad):
    wide = tokens.astype(jnp.float32)
    inv_rms = lax.rsqrt(lax.optimization_barrier(jnp.mean(wide * wide, axis=1, keepdims=True)) + eps)
    unit = wide * inv_rms
    normed = (unit * norm_gain).astype(jnp.bfloat16)
    blocks = D // BLOCK
    weight = (weight_codes.astype(jnp.float32).reshape(blocks, BLOCK, KV) * block_scales[:, None, :]).reshape(D, KV).astype(jnp.bfloat16)
    keys = jnp.dot(normed, weight, preferred_element_type=jnp.float32).astype(jnp.bfloat16)
    count = N_REP * N_GRP
    summed = lax.dot_general(normed, key_grad, (((0,), (0,)), ((), ())), preferred_element_type=jnp.float32)
    weight_grad = summed / count
    normed_grad = lax.dot_general(key_grad, weight, (((1,), (1,)), ((), ())), preferred_element_type=jnp.float32)
    gain_grad = lax.optimization_barrier(jnp.sum(normed_grad * unit, axis=0)) / count
    scaled_grad = normed_grad * norm_gain
    tokens_grad = (inv_rms * (scaled_grad - unit * lax.optimization_barrier(jnp.mean(scaled_grad * unit, axis=1, keepdims=True)))).astype(jnp.bfloat16)
    return (keys, tokens_grad, weight_grad, gain_grad)
```

```python
import jax
import jax.numpy as jnp
from jax import lax
from jax.sharding import Mesh, PartitionSpec as P

eps = 1e-05
AXES = ("zh", "x", "core", "y", "zl")
SIZES = (4, 4, 2, 4, 4)
Z = ("zh", "zl")
f32, bf16 = jnp.float32, jnp.bfloat16


def exchange(blocks, axes):
    return lax.all_to_all(blocks, axes, 0, 0, tiled=False)


def everywhere(block, axes):
    peers = lax.axis_size(axes)
    return exchange(jnp.broadcast_to(block[None], (peers,) + block.shape), axes)


def swap(block):
    return lax.ppermute(block, "core", [(0, 1), (1, 0)])


def along_z(block, by_core):
    pairs = []
    for core in range(2):
        for z in range(16):
            target = (z + by_core[core]) % 16
            pairs.append(((z // 4 * 2 + core) * 4 + z % 4, (target // 4 * 2 + core) * 4 + target % 4))
    return lax.ppermute(block, ("zh", "core", "zl"), pairs)


def local(tokens, norm_gain, weight_codes, block_scales, key_grad):
    core = lax.axis_index("core")
    x = lax.axis_index("x")
    zl = lax.axis_index("zl")
    devices = 512
    half = 256
    wide = tokens.astype(f32)
    inv_rms = lax.rsqrt(jnp.mean(wide * wide, axis=1, keepdims=True) + eps)
    unit = wide * inv_rms
    normed = (unit * norm_gain).astype(bf16)

    def columns(array, which):
        return lax.dynamic_slice_in_dim(array, which * half, half, 1)

    def product(which):
        part = lax.dot_general(
            normed, columns(key_grad, which), (((0,), (0,)), ((), ())), preferred_element_type=f32
        )
        return part.reshape(4, 4, 4, 32, half).transpose(0, 2, 1, 3, 4).reshape(16, 4, 32, half)

    theirs = product(1 - core).astype(bf16)
    got = swap(theirs)
    codes = columns(weight_codes, core).astype(f32)
    weight = (codes * columns(block_scales, core)).astype(bf16)
    weight, _ = lax.optimization_barrier((weight, theirs))
    shard_y = everywhere(weight, "y")

    pair = (product(core) + got.astype(f32)).astype(bf16)
    square = exchange(pair, ("y", "x"))

    below = along_z(shard_y, (1, 1))
    above = along_z(shard_y, (-1, -1))
    across = along_z(shard_y, (2, -2))
    stack = jnp.stack([shard_y, above, across, below])

    partial = jnp.sum(square.astype(f32), axis=0)
    y = lax.axis_index("y")
    rows = lax.dynamic_slice(stack, (0, y, x * 32, 0), (4, 1, 32, half))[:, 0]
    mine = jnp.roll(rows, zl, axis=0)
    gain_part = jnp.sum(mine.astype(f32) * partial, axis=2)
    high = gain_part.astype(bf16)
    low = (gain_part - high.astype(f32)).astype(bf16)
    extra = jnp.zeros((32, 128), bf16).at[:, 0:4].set(high.T).at[:, 4:8].set(low.T)
    payload = jnp.concatenate(
        [partial.astype(bf16), jnp.broadcast_to(extra[None], (4, 32, 128))], axis=2
    )
    line = exchange(jnp.broadcast_to(payload[None], (4, 4, 32, 384)).reshape(16, 32, 384), Z)
    total = jnp.sum(line.astype(f32), axis=0)
    gain_rows = (total[:, 256:260] + total[:, 260:264]).T
    gain_all = everywhere(jnp.pad(gain_rows, ((0, 4), (0, 96))), ("y", "x", "core"))
    rows_all = everywhere(total[:, :256].astype(bf16), ("x", "core"))
    weight_grad = (
        rows_all.reshape(4, 2, 32, half).transpose(0, 2, 1, 3).reshape(128, 512).astype(f32) / devices
    )
    gain_sum = gain_all[:, :4, :32].reshape(4, 4, 2, 4, 32).sum(2)
    gain_grad = gain_sum.transpose(0, 2, 1, 3).reshape(2048) / (norm_gain * devices)

    other = swap(stack)
    left = jnp.where(core == 0, stack, other)
    right = jnp.where(core == 0, other, stack)
    whole = jnp.concatenate([left, right], axis=3)
    full = jnp.roll(whole, zl, axis=0).transpose(1, 0, 2, 3).reshape(2048, 512)
    keys = jnp.dot(normed, full, preferred_element_type=f32).astype(bf16)
    normed_grad = lax.dot_general(
        key_grad, full, (((1,), (1,)), ((), ())), preferred_element_type=f32
    )
    scaled_grad = normed_grad * norm_gain
    tokens_grad = (
        inv_rms * (scaled_grad - unit * jnp.mean(scaled_grad * unit, axis=1, keepdims=True))
    ).astype(bf16)
    return (keys, tokens_grad, weight_grad, gain_grad)


def solution(mesh):
    fine = Mesh(mesh.devices.reshape(SIZES), AXES)
    everyone = P(AXES, None)
    group = P(("y", "zl"), None)
    in_specs = (everyone, P(), group, group, everyone)
    out_specs = (everyone, everyone, group, P())
    return jax.shard_map(local, mesh=fine, in_specs=in_specs, out_specs=out_specs, check_vma=False)
```

```python
import functools

import jax
import jax.numpy as jnp
from jax import lax
from jax.experimental import pallas as pl
from jax.experimental.pallas import tpu as pltpu
from jax.sharding import Mesh, PartitionSpec as P

eps = 1e-05
AXES = ("zh", "x", "core", "y", "zl")
SIZES = (4, 4, 2, 4, 4)
Z = ("zh", "zl")
DEVICES = 512
HALF = 256
f32, bf16 = jnp.float32, jnp.bfloat16
VMEM = pl.BlockSpec(memory_space=pltpu.VMEM)
SMEM = pl.BlockSpec(memory_space=pltpu.SMEM)
ANY = pl.BlockSpec(memory_space=pl.ANY)
PARAMS = pltpu.CompilerParams(vmem_limit_bytes=40 * 1024 * 1024)


def exchange(blocks, axes):
    return lax.all_to_all(blocks, axes, 0, 0, tiled=False)


def swap(block):
    return lax.ppermute(block, "core", [(0, 1), (1, 0)])


def along_y(block, step):
    return lax.ppermute(block, "y", [(y, (y + step) % 4) for y in range(4)])


def along_z(block, step):
    pairs = []
    for z in range(16):
        for x in range(4):
            for core in range(2):
                to = (z + step(x, core)) % 16
                pairs.append(
                    (((z // 4 * 4 + x) * 2 + core) * 4 + z % 4, ((to // 4 * 4 + x) * 2 + core) * 4 + to % 4)
                )
    return lax.ppermute(block, ("zh", "x", "core", "zl"), pairs)


def contract_rows(a, b):
    return lax.dot_general(a, b, (((0,), (0,)), ((), ())), preferred_element_type=f32)


def put_product(normed, grad, out, dtype):
    for k in range(8):
        part = contract_rows(normed[:, k * HALF : (k + 1) * HALF], grad)
        for sub in range(16):
            pair = jnp.concatenate(
                [part[sub * 8 : sub * 8 + 8], part[128 + sub * 8 : 136 + sub * 8]], axis=0
            )
            out[sub, :, k * HALF : (k + 1) * HALF] = pair.astype(dtype)


def norm_kernel(place, tokens, norm_gain, key_grad, normed, inv_rms, theirs):
    wide = tokens[...].astype(f32)
    inv = lax.rsqrt(jnp.mean(wide * wide, axis=1, keepdims=True) + eps)
    inv_rms[...] = jnp.broadcast_to(inv, inv_rms.shape)
    normed[...] = (wide * inv * norm_gain[...]).astype(bf16)
    start = pl.multiple_of((1 - place[0]) * HALF, HALF)
    put_product(normed, key_grad[:, pl.ds(start, HALF)], theirs, bf16)


def mine_kernel(place, normed, key_grad, mine):
    start = pl.multiple_of(place[0] * HALF, HALF)
    put_product(normed, key_grad[:, pl.ds(start, HALF)], mine, f32)


def pair_kernel(mine, got, rows, out):
    for sub in range(16):
        out[sub, :, :2048] = (mine[sub] + got[sub].astype(f32)).astype(bf16)
        own = rows[sub * 8 : sub * 8 + 8, :].astype(f32)
        out[sub, :, 2048:] = jnp.concatenate([own[:, :128], own[:, 128:]], axis=0).astype(bf16)


def square_kernel(place, square, out, shards, products):
    zl = place[3]
    for k in range(8):
        cols = slice(k * HALF, (k + 1) * HALF)
        total = square[0, :, cols].astype(f32)
        for sender in range(1, 16):
            total += square[sender, :, cols].astype(f32)
        shards[2 * k] = total[:8]
        shards[2 * k + 1] = total[8:]
    for sender in range(16):
        shard = sender // 4 * 4 + lax.rem(zl + sender % 4, 4)
        packed = square[sender, :, 2048:].astype(f32)
        rows = jnp.concatenate([packed[:8], packed[8:]], axis=1)
        products[shard] = shards[shard] * rows
    gain = lax.dot_general(
        jnp.ones((16, HALF), f32),
        products[...].reshape(128, HALF),
        (((1,), (1,)), ((), ())),
        preferred_element_type=f32,
        precision=lax.Precision.HIGHEST,
    )
    high = gain.astype(bf16).astype(f32)
    row = lax.broadcasted_iota(jnp.int32, (16, 128), 0)
    gains = jnp.where(row == 0, high, jnp.where(row == 1, gain - high, 0.0)).astype(bf16)
    for target in range(4):
        first = jnp.concatenate([shards[target], shards[4 + target]], axis=0).astype(bf16)
        second = jnp.concatenate([shards[8 + target], shards[12 + target]], axis=0).astype(bf16)
        for zh in range(4):
            z = zh * 4 + target
            out[z, :, :HALF] = first
            out[z, :, HALF : 2 * HALF] = second
            out[z, :, 2 * HALF :] = gains


def line_kernel(line, out):
    total = line[0].astype(f32)
    for sender in range(1, 16):
        total += line[sender].astype(f32)
    gain = total[0:1, 512:] + total[1:2, 512:]
    high = gain.astype(bf16).astype(f32)
    both = jnp.concatenate([high, gain - high], axis=1)
    row = lax.broadcasted_iota(jnp.int32, (8, HALF), 0)
    gains = jnp.where(row == 0, jnp.broadcast_to(both, (8, HALF)), 0.0)
    for y in range(4):
        rows = total[y % 2 * 8 : y % 2 * 8 + 8, y // 2 * HALF : (y // 2 + 1) * HALF]
        block = jnp.concatenate([rows, gains], axis=0).astype(bf16)
        for peer in range(8):
            out[y * 8 + peer] = block


def last_kernel(blocks, norm_gain, weight_grad, gain_grad):
    rows_of = []
    for sub in range(16):
        gains = None
        for core in range(2):
            block = blocks[sub * 2 + core].astype(f32)
            weight_grad[sub * 8 : sub * 8 + 8, core * HALF : (core + 1) * HALF] = block[:8] / DEVICES
            gain = block[8:9, :128] + block[8:9, 128:]
            gains = gain if gains is None else gains + gain
        rows_of.append(gains)
    sums = jnp.concatenate(rows_of, axis=0)
    lane = lax.broadcasted_iota(jnp.int32, (16, 128), 1)
    sub = lax.broadcasted_iota(jnp.int32, (16, 128), 0)
    spread = (
        lax.broadcasted_iota(jnp.int32, (128, 128), 0) % 8
        == lax.broadcasted_iota(jnp.int32, (128, 128), 1) % 8
    ).astype(f32)
    stacked = jnp.concatenate(
        [jnp.where(lane // 8 == shard, sums, 0.0) for shard in range(16)], axis=0
    )
    moved = lax.dot_general(
        stacked, spread, (((1,), (0,)), ((), ())), preferred_element_type=f32,
        precision=lax.Precision.HIGHEST,
    )
    for shard in range(16):
        block = moved[shard * 16 : shard * 16 + 16]
        gain_grad[shard : shard + 1, :] = jnp.sum(
            jnp.where(lane // 8 == sub, block, 0.0), axis=0, keepdims=True
        ) / (norm_gain[shard : shard + 1, :] * DEVICES)


def token_kernel(place, tokens, inv_rms, norm_gain, key_grad, *rest):
    pieces, (keys, tokens_grad, weight, sem) = rest[:8], rest[8:]
    core, y, zl = place[0], place[2], place[3]
    copies = []
    for step in range(4):
        for side in range(2):
            column = core * HALF if side == 0 else (1 - core) * HALF
            for j in range(4):
                row = (lax.rem(y + step, 4) * 4 + lax.rem(zl + j, 4)) * 128
                copies.append(
                    pltpu.make_async_copy(
                        pieces[step * 2 + side].at[j],
                        weight.at[pl.ds(pl.multiple_of(row, 128), 128), pl.ds(pl.multiple_of(column, HALF), HALF)],
                        sem.at[len(copies)],
                    )
                )
    for copy in copies:
        copy.start()
    for copy in copies:
        copy.wait()
    for rows in (slice(0, 96), slice(96, 192)):
        inv = inv_rms[rows, 0:1]
        unit = tokens[rows, :].astype(f32) * inv
        normed = (unit * norm_gain[...]).astype(bf16)
        keys[rows, :] = jnp.dot(normed, weight[...], preferred_element_type=f32).astype(bf16)
        scaled = norm_gain[...] * lax.dot_general(
            key_grad[rows, :], weight[...], (((1,), (1,)), ((), ())), preferred_element_type=f32
        )
        mean = jnp.mean(scaled * unit, axis=1, keepdims=True)
        tokens_grad[rows, :] = (inv * (scaled - unit * mean)).astype(bf16)


def call(kernel, outs, ins, args, scratch=(), flops=0, **kw):
    moved = sum(a.size * a.dtype.itemsize for a in args)
    return pl.pallas_call(
        kernel,
        out_shape=[jax.ShapeDtypeStruct(s, d) for s, d in outs],
        in_specs=ins,
        out_specs=[VMEM] * len(outs),
        scratch_shapes=list(scratch),
        compiler_params=PARAMS,
        cost_estimate=pl.CostEstimate(flops=flops, bytes_accessed=2 * moved, transcendentals=0),
    )(*args)


def local(tokens, norm_gain, weight_codes, block_scales, key_grad):
    core = lax.axis_index("core")
    place = jnp.stack(
        [core, lax.axis_index("x"), lax.axis_index("y"), lax.axis_index("zl")]
    ).astype(jnp.int32)
    gain_row = norm_gain.reshape(1, 2048)

    codes = lax.dynamic_slice_in_dim(weight_codes, core * HALF, HALF, 1)
    scales = lax.dynamic_slice_in_dim(block_scales, core * HALF, HALF, 1)
    shard = (codes.astype(f32) * scales).astype(bf16)
    gain_rows = along_z(shard, lambda x, core: (0, -1, -2, 1)[x])

    normed, inv_rms, theirs = call(
        norm_kernel,
        [((192, 2048), bf16), ((192, 128), f32), ((16, 16, 2048), bf16)],
        [SMEM, VMEM, VMEM, VMEM],
        (place, tokens, gain_row, key_grad),
        flops=2 * 192 * 2048 * 256,
    )
    got = swap(theirs)
    (mine,) = call(
        mine_kernel,
        [((16, 16, 2048), f32)],
        [SMEM, VMEM, VMEM],
        (place, normed, key_grad),
        flops=2 * 192 * 2048 * 256,
    )
    (pair,) = call(pair_kernel, [((16, 16, 2176), bf16)], [VMEM] * 3, (mine, got, gain_rows))
    square = exchange(pair, ("y", "x"))

    shard_late, _ = lax.optimization_barrier((shard, pair))
    above = along_z(shard_late, lambda x, core: -1)
    across = along_z(shard_late, lambda x, core: (2, -2)[core])
    below = along_z(shard_late, lambda x, core: 1)
    stack = jnp.stack([shard, above, across, below])

    (payload,) = call(
        square_kernel,
        [((16, 16, 640), bf16)],
        [SMEM, VMEM],
        (place, square),
        scratch=[pltpu.VMEM((16, 8, HALF), f32), pltpu.VMEM((16, 8, HALF), f32)],
    )
    line = exchange(payload, Z)

    stack_late, _ = lax.optimization_barrier((stack, payload))
    pieces = []
    for step in range(4):
        piece = stack if step == 0 else along_y(stack_late, -step)
        pieces += [piece, swap(piece)]
    (blocks,) = call(line_kernel, [((32, 16, HALF), bf16)], [VMEM], (line,))
    blocks = exchange(blocks, ("y", "x", "core"))
    keys, tokens_grad = call(
        token_kernel,
        [((192, 512), bf16), ((192, 2048), bf16)],
        [SMEM, VMEM, VMEM, VMEM, VMEM] + [ANY] * 8,
        (place, tokens, inv_rms, gain_row, key_grad, *pieces),
        scratch=[pltpu.VMEM((2048, 512), bf16), pltpu.SemaphoreType.DMA((32,))],
        flops=4 * 192 * 2048 * 512,
    )
    weight_grad, gain_grad = call(
        last_kernel,
        [((128, 512), f32), ((16, 128), f32)],
        [VMEM] * 2,
        (blocks, norm_gain.reshape(16, 128)),
    )
    return keys, tokens_grad, weight_grad, gain_grad.reshape(2048)


def solution(mesh):
    fine = Mesh(mesh.devices.reshape(SIZES), AXES)
    everyone = P(AXES, None)
    group = P(("y", "zl"), None)
    in_specs = (everyone, P(), group, group, everyone)
    out_specs = (everyone, everyone, group, P())
    return jax.shard_map(local, mesh=fine, in_specs=in_specs, out_specs=out_specs, check_vma=False)
```

```python
import functools

import jax
import jax.numpy as jnp
from jax import lax
from jax.experimental import pallas as pl
from jax.experimental.pallas import tpu as pltpu
from jax.sharding import Mesh, PartitionSpec as P

eps = 1e-05
AXES = ("zh", "x", "core", "y", "zl")
SIZES = (4, 4, 2, 4, 4)
Z = ("zh", "zl")
DEVICES = 512
HALF = 256
f32, bf16 = jnp.float32, jnp.bfloat16
VMEM = pl.BlockSpec(memory_space=pltpu.VMEM)
SMEM = pl.BlockSpec(memory_space=pltpu.SMEM)
ANY = pl.BlockSpec(memory_space=pl.ANY)
HBM = pl.BlockSpec(memory_space=pltpu.HBM)
PARAMS = pltpu.CompilerParams(vmem_limit_bytes=40 * 1024 * 1024)


def in_hbm(array):
    return pltpu.with_memory_space_constraint(array, pltpu.HBM)


def exchange(blocks, axes):
    return lax.all_to_all(blocks, axes, 0, 0, tiled=False)


def swap(block):
    return lax.ppermute(block, "core", [(0, 1), (1, 0)])


def along_y(block, step):
    return lax.ppermute(block, "y", [(y, (y + step) % 4) for y in range(4)])


def along_z(block, step):
    pairs = []
    for z in range(16):
        for x in range(4):
            for core in range(2):
                to = (z + step(x, core)) % 16
                pairs.append(
                    (((z // 4 * 4 + x) * 2 + core) * 4 + z % 4, ((to // 4 * 4 + x) * 2 + core) * 4 + to % 4)
                )
    return lax.ppermute(block, ("zh", "x", "core", "zl"), pairs)


def contract_rows(a, b):
    return lax.dot_general(a, b, (((0,), (0,)), ((), ())), preferred_element_type=f32)


def put_product(normed, grad, out, dtype):
    for k in range(8):
        part = contract_rows(normed[:, k * HALF : (k + 1) * HALF], grad)
        for sub in range(16):
            pair = jnp.concatenate(
                [part[sub * 8 : sub * 8 + 8], part[128 + sub * 8 : 136 + sub * 8]], axis=0
            )
            out[sub, :, k * HALF : (k + 1) * HALF] = pair.astype(dtype)


def norm_kernel(place, tokens_at, gain_at, grad_at, normed, inv_rms, theirs, tokens, norm_gain, key_grad, sem):
    copies = [
        pltpu.make_async_copy(source, target, sem.at[i])
        for i, (source, target) in enumerate(
            ((tokens_at, tokens), (gain_at, norm_gain), (grad_at, key_grad))
        )
    ]
    for copy in copies:
        copy.start()
    for copy in copies:
        copy.wait()
    wide = tokens[...].astype(f32)
    inv = lax.rsqrt(jnp.mean(wide * wide, axis=1, keepdims=True) + eps)
    inv_rms[...] = jnp.broadcast_to(inv, inv_rms.shape)
    normed[...] = (wide * inv * norm_gain[...]).astype(bf16)
    start = pl.multiple_of((1 - place[0]) * HALF, HALF)
    put_product(normed, key_grad[:, pl.ds(start, HALF)], theirs, bf16)


def mine_kernel(place, normed, key_grad, mine):
    start = pl.multiple_of(place[0] * HALF, HALF)
    put_product(normed, key_grad[:, pl.ds(start, HALF)], mine, f32)


def pair_kernel(mine, got, rows, out):
    for sub in range(16):
        out[sub, :, :2048] = (mine[sub] + got[sub].astype(f32)).astype(bf16)
        own = rows[sub * 8 : sub * 8 + 8, :].astype(f32)
        out[sub, :, 2048:] = jnp.concatenate([own[:, :128], own[:, 128:]], axis=0).astype(bf16)


def square_kernel(place, square, out, shards, products):
    zl = place[3]
    for k in range(8):
        cols = slice(k * HALF, (k + 1) * HALF)
        total = square[0, :, cols].astype(f32)
        for sender in range(1, 16):
            total += square[sender, :, cols].astype(f32)
        shards[2 * k] = total[:8]
        shards[2 * k + 1] = total[8:]
    for sender in range(16):
        shard = sender // 4 * 4 + lax.rem(zl + sender % 4, 4)
        packed = square[sender, :, 2048:].astype(f32)
        rows = jnp.concatenate([packed[:8], packed[8:]], axis=1)
        products[shard] = shards[shard] * rows
    gain = lax.dot_general(
        jnp.ones((16, HALF), f32),
        products[...].reshape(128, HALF),
        (((1,), (1,)), ((), ())),
        preferred_element_type=f32,
        precision=lax.Precision.HIGHEST,
    )
    high = gain.astype(bf16).astype(f32)
    row = lax.broadcasted_iota(jnp.int32, (16, 128), 0)
    gains = jnp.where(row == 0, high, jnp.where(row == 1, gain - high, 0.0)).astype(bf16)
    for target in range(4):
        first = jnp.concatenate([shards[target], shards[4 + target]], axis=0).astype(bf16)
        second = jnp.concatenate([shards[8 + target], shards[12 + target]], axis=0).astype(bf16)
        for zh in range(4):
            z = zh * 4 + target
            out[z, :, :HALF] = first
            out[z, :, HALF : 2 * HALF] = second
            out[z, :, 2 * HALF :] = gains


def line_kernel(line, out):
    total = line[0].astype(f32)
    for sender in range(1, 16):
        total += line[sender].astype(f32)
    gain = total[0:1, 512:] + total[1:2, 512:]
    high = gain.astype(bf16).astype(f32)
    both = jnp.concatenate([high, gain - high], axis=1)
    row = lax.broadcasted_iota(jnp.int32, (8, HALF), 0)
    gains = jnp.where(row == 0, jnp.broadcast_to(both, (8, HALF)), 0.0)
    for y in range(4):
        rows = total[y % 2 * 8 : y % 2 * 8 + 8, y // 2 * HALF : (y // 2 + 1) * HALF]
        block = jnp.concatenate([rows, gains], axis=0).astype(bf16)
        for peer in range(8):
            out[y * 8 + peer] = block


def last_kernel(blocks, norm_gain, weight_grad, gain_grad):
    rows_of = []
    for sub in range(16):
        gains = None
        for core in range(2):
            block = blocks[sub * 2 + core].astype(f32)
            weight_grad[sub * 8 : sub * 8 + 8, core * HALF : (core + 1) * HALF] = block[:8] / DEVICES
            gain = block[8:9, :128] + block[8:9, 128:]
            gains = gain if gains is None else gains + gain
        rows_of.append(gains)
    sums = jnp.concatenate(rows_of, axis=0)
    lane = lax.broadcasted_iota(jnp.int32, (16, 128), 1)
    sub = lax.broadcasted_iota(jnp.int32, (16, 128), 0)
    spread = (
        lax.broadcasted_iota(jnp.int32, (128, 128), 0) % 8
        == lax.broadcasted_iota(jnp.int32, (128, 128), 1) % 8
    ).astype(f32)
    stacked = jnp.concatenate(
        [jnp.where(lane // 8 == shard, sums, 0.0) for shard in range(16)], axis=0
    )
    moved = lax.dot_general(
        stacked, spread, (((1,), (0,)), ((), ())), preferred_element_type=f32,
        precision=lax.Precision.HIGHEST,
    )
    for shard in range(16):
        block = moved[shard * 16 : shard * 16 + 16]
        gain_grad[shard : shard + 1, :] = jnp.sum(
            jnp.where(lane // 8 == sub, block, 0.0), axis=0, keepdims=True
        ) / (norm_gain[shard : shard + 1, :] * DEVICES)


def token_kernel(place, tokens, inv_rms, norm_gain, key_grad, *rest):
    pieces, (keys, tokens_grad, weight, sem) = rest[:8], rest[8:]
    core, y, zl = place[0], place[2], place[3]
    copies = []
    for step in range(4):
        for side in range(2):
            column = core * HALF if side == 0 else (1 - core) * HALF
            for j in range(4):
                row = (lax.rem(y + step, 4) * 4 + lax.rem(zl + j, 4)) * 128
                copies.append(
                    pltpu.make_async_copy(
                        pieces[step * 2 + side].at[j],
                        weight.at[pl.ds(pl.multiple_of(row, 128), 128), pl.ds(pl.multiple_of(column, HALF), HALF)],
                        sem.at[len(copies)],
                    )
                )
    for copy in copies:
        copy.start()
    for copy in copies:
        copy.wait()
    for rows in (slice(0, 96), slice(96, 192)):
        inv = inv_rms[rows, 0:1]
        unit = tokens[rows, :].astype(f32) * inv
        normed = (unit * norm_gain[...]).astype(bf16)
        keys[rows, :] = jnp.dot(normed, weight[...], preferred_element_type=f32).astype(bf16)
        scaled = norm_gain[...] * lax.dot_general(
            key_grad[rows, :], weight[...], (((1,), (1,)), ((), ())), preferred_element_type=f32
        )
        mean = jnp.mean(scaled * unit, axis=1, keepdims=True)
        tokens_grad[rows, :] = (inv * (scaled - unit * mean)).astype(bf16)


def call(kernel, outs, ins, args, scratch=(), flops=0, **kw):
    moved = sum(a.size * a.dtype.itemsize for a in args)
    return pl.pallas_call(
        kernel,
        out_shape=[jax.ShapeDtypeStruct(s, d) for s, d in outs],
        in_specs=ins,
        out_specs=[VMEM] * len(outs),
        scratch_shapes=list(scratch),
        compiler_params=PARAMS,
        cost_estimate=pl.CostEstimate(flops=flops, bytes_accessed=2 * moved, transcendentals=0),
    )(*args)


def local(tokens, norm_gain, weight_codes, block_scales, key_grad):
    core = lax.axis_index("core")
    place = jnp.stack(
        [core, lax.axis_index("x"), lax.axis_index("y"), lax.axis_index("zl")]
    ).astype(jnp.int32)
    gain_row = norm_gain.reshape(1, 2048)

    codes = lax.dynamic_slice_in_dim(weight_codes, core * HALF, HALF, 1)
    scales = lax.dynamic_slice_in_dim(block_scales, core * HALF, HALF, 1)
    shard = (codes.astype(f32) * scales).astype(bf16)
    gain_rows = along_z(shard, lambda x, core: (0, -1, -2, 1)[x])

    tokens_first, _ = lax.optimization_barrier((tokens, shard))
    normed, inv_rms, theirs = call(
        norm_kernel,
        [((192, 2048), bf16), ((192, 128), f32), ((16, 16, 2048), bf16)],
        [SMEM, HBM, HBM, HBM],
        (place, in_hbm(tokens_first), in_hbm(gain_row), in_hbm(key_grad)),
        scratch=[
            pltpu.VMEM((192, 2048), bf16),
            pltpu.VMEM((1, 2048), f32),
            pltpu.VMEM((192, 512), bf16),
            pltpu.SemaphoreType.DMA((3,)),
        ],
        flops=2 * 192 * 2048 * 256,
    )
    got = swap(theirs)
    (mine,) = call(
        mine_kernel,
        [((16, 16, 2048), f32)],
        [SMEM, VMEM, VMEM],
        (place, normed, key_grad),
        flops=2 * 192 * 2048 * 256,
    )
    (pair,) = call(pair_kernel, [((16, 16, 2176), bf16)], [VMEM] * 3, (mine, got, gain_rows))
    square = exchange(pair, ("y", "x"))

    shard_late, _ = lax.optimization_barrier((shard, pair))
    above = along_z(shard_late, lambda x, core: -1)
    across = along_z(shard_late, lambda x, core: (2, -2)[core])
    below = along_z(shard_late, lambda x, core: 1)
    square, above, across, below = lax.optimization_barrier((square, above, across, below))
    stack = jnp.stack([shard, above, across, below])

    (payload,) = call(
        square_kernel,
        [((16, 16, 640), bf16)],
        [SMEM, VMEM],
        (place, square),
        scratch=[pltpu.VMEM((16, 8, HALF), f32), pltpu.VMEM((16, 8, HALF), f32)],
    )
    line = exchange(payload, Z)

    stack_late, _ = lax.optimization_barrier((stack, payload))
    pieces = []
    for step in range(4):
        piece = stack if step == 0 else along_y(stack_late, -step)
        pieces += [piece, swap(piece)]
    line, *pieces = lax.optimization_barrier((line, *pieces))
    (blocks,) = call(line_kernel, [((32, 16, HALF), bf16)], [VMEM], (line,))
    blocks = exchange(blocks, ("y", "x", "core"))
    keys, tokens_grad = call(
        token_kernel,
        [((192, 512), bf16), ((192, 2048), bf16)],
        [SMEM, VMEM, VMEM, VMEM, VMEM] + [ANY] * 8,
        (place, tokens, inv_rms, gain_row, key_grad, *pieces),
        scratch=[pltpu.VMEM((2048, 512), bf16), pltpu.SemaphoreType.DMA((32,))],
        flops=4 * 192 * 2048 * 512,
    )
    weight_grad, gain_grad = call(
        last_kernel,
        [((128, 512), f32), ((16, 128), f32)],
        [VMEM] * 2,
        (blocks, norm_gain.reshape(16, 128)),
    )
    return keys, tokens_grad, weight_grad, gain_grad.reshape(2048)


def solution(mesh):
    fine = Mesh(mesh.devices.reshape(SIZES), AXES)
    everyone = P(AXES, None)
    group = P(("y", "zl"), None)
    in_specs = (everyone, P(), group, group, everyone)
    out_specs = (everyone, everyone, group, P())
    return jax.shard_map(local, mesh=fine, in_specs=in_specs, out_specs=out_specs, check_vma=False)
```

```python
import functools

import jax
import jax.numpy as jnp
from jax import lax
from jax.experimental import pallas as pl
from jax.experimental.pallas import tpu as pltpu
from jax.sharding import Mesh, PartitionSpec as P

eps = 1e-05
AXES = ("zh", "x", "core", "y", "zl")
SIZES = (4, 4, 2, 4, 4)
Z = ("zh", "zl")
DEVICES = 512
HALF = 256
f32, bf16 = jnp.float32, jnp.bfloat16
VMEM = pl.BlockSpec(memory_space=pltpu.VMEM)
SMEM = pl.BlockSpec(memory_space=pltpu.SMEM)
ANY = pl.BlockSpec(memory_space=pl.ANY)
HBM = pl.BlockSpec(memory_space=pltpu.HBM)
PARAMS = pltpu.CompilerParams(vmem_limit_bytes=40 * 1024 * 1024)


def in_hbm(array):
    return pltpu.with_memory_space_constraint(array, pltpu.HBM)


def exchange(blocks, axes):
    return lax.all_to_all(blocks, axes, 0, 0, tiled=False)


def swap(block):
    return lax.ppermute(block, "core", [(0, 1), (1, 0)])


def along_y(block, step):
    return lax.ppermute(block, "y", [(y, (y + step) % 4) for y in range(4)])


def along_z(block, step):
    pairs = []
    for z in range(16):
        for x in range(4):
            for core in range(2):
                to = (z + step(x, core)) % 16
                pairs.append(
                    (((z // 4 * 4 + x) * 2 + core) * 4 + z % 4, ((to // 4 * 4 + x) * 2 + core) * 4 + to % 4)
                )
    return lax.ppermute(block, ("zh", "x", "core", "zl"), pairs)


def contract_rows(a, b):
    return lax.dot_general(a, b, (((0,), (0,)), ((), ())), preferred_element_type=f32)


def put_product(normed, grad, out, dtype):
    for part_at in range(8):
        y, first = part_at // 2, part_at % 2 * 2
        part = contract_rows(normed[:, part_at * HALF : (part_at + 1) * HALF], grad).astype(dtype)
        for x in range(4):
            for k in range(4):
                row = k // 2 * 128 + x * 32 + k % 2 * 16
                column = (first * 2 + k) * HALF
                out[y * 4 + x, :, column : column + HALF] = part[row : row + 16]


def norm_kernel(place, tokens_at, gain_at, grad_at, normed, inv_rms, theirs, tokens, norm_gain, key_grad, sem):
    copies = [
        pltpu.make_async_copy(source, target, sem.at[i])
        for i, (source, target) in enumerate(
            ((tokens_at, tokens), (gain_at, norm_gain), (grad_at, key_grad))
        )
    ]
    for copy in copies:
        copy.start()
    for copy in copies:
        copy.wait()
    wide = tokens[...].astype(f32)
    inv = lax.rsqrt(jnp.mean(wide * wide, axis=1, keepdims=True) + eps)
    inv_rms[...] = jnp.broadcast_to(inv, inv_rms.shape)
    normed[...] = (wide * inv * norm_gain[...]).astype(bf16)
    start = pl.multiple_of((1 - place[0]) * HALF, HALF)
    put_product(normed, key_grad[:, pl.ds(start, HALF)], theirs, bf16)


def mine_kernel(place, normed, key_grad, mine):
    start = pl.multiple_of(place[0] * HALF, HALF)
    put_product(normed, key_grad[:, pl.ds(start, HALF)], mine, f32)


def pair_kernel(mine, got, out):
    for peer in range(16):
        out[peer] = (mine[peer] + got[peer].astype(f32)).astype(bf16)


def two_rows(value):
    high = value.astype(bf16).astype(f32)
    row = lax.broadcasted_iota(jnp.int32, (16, 128), 0)
    return jnp.where(row == 0, high, jnp.where(row == 1, value - high, 0.0)).astype(bf16)


def square_kernel(place, square, shard, above, across, below, out, shards, products):
    x, zl = place[1], place[3]
    for k in range(8):
        cols = slice(k * HALF, (k + 1) * HALF)
        total = square[0, :, cols].astype(f32)
        for sender in range(1, 16):
            total += square[sender, :, cols].astype(f32)
        shards[k // 2, k % 2 * 16 : k % 2 * 16 + 16] = total
    for j, piece in enumerate((shard, above, across, below)):
        which = lax.rem(zl + j, 4)
        rows = piece[pl.ds(pl.multiple_of(x * 32, 32), 32), :].astype(f32)
        products[which] = shards[which] * rows
    gain = lax.dot_general(
        jnp.ones((16, HALF), f32),
        products[...].reshape(128, HALF),
        (((1,), (1,)), ((), ())),
        preferred_element_type=f32,
        precision=lax.Precision.HIGHEST,
    )
    gains = two_rows(gain)
    for target in range(4):
        rows = shards[target].astype(bf16)
        for zh in range(4):
            z = zh * 4 + target
            out[z, :, :HALF] = rows[:16]
            out[z, :, HALF : 2 * HALF] = rows[16:]
            out[z, :, 2 * HALF :] = gains


def line_kernel(line, out):
    total = line[0].astype(f32)
    for sender in range(1, 16):
        total += line[sender].astype(f32)
    gains = two_rows(jnp.broadcast_to(total[0:1, 512:] + total[1:2, 512:], (16, 128)))
    rows = total[:, :512].astype(bf16)
    for peer in range(32):
        out[peer, :, :512] = rows
        out[peer, :, 512:] = gains


def last_kernel(place, blocks, norm_gain, weight_grad, gain_grad):
    y = place[2]
    for x in range(4):
        for core in range(2):
            block = blocks[y * 8 + x * 2 + core].astype(f32) / DEVICES
            for k in range(2):
                weight_grad[x * 32 + k * 16 : x * 32 + k * 16 + 16, core * HALF : (core + 1) * HALF] = block[
                    :, k * HALF : (k + 1) * HALF
                ]
    rows_of = []
    for peer in range(16):
        gains = blocks[peer * 2, :, 512:].astype(f32) + blocks[peer * 2 + 1, :, 512:].astype(f32)
        rows_of.append(gains[0:1] + gains[1:2])
    sums = jnp.concatenate(rows_of, axis=0)
    lane = lax.broadcasted_iota(jnp.int32, (16, 128), 1)
    peer = lax.broadcasted_iota(jnp.int32, (16, 128), 0)
    spread = (
        lax.broadcasted_iota(jnp.int32, (128, 128), 0) % 32
        == lax.broadcasted_iota(jnp.int32, (128, 128), 1) % 32
    ).astype(f32)
    stacked = jnp.concatenate([jnp.where(lane // 32 == zl, sums, 0.0) for zl in range(4)], axis=0)
    moved = lax.dot_general(
        stacked, spread, (((1,), (0,)), ((), ())), preferred_element_type=f32,
        precision=lax.Precision.HIGHEST,
    )
    for row in range(4):
        for zl in range(4):
            picked = jnp.where(peer == row * 4 + lane // 32, moved[zl * 16 : zl * 16 + 16], 0.0)
            at = row * 4 + zl
            gain_grad[at : at + 1, :] = jnp.sum(picked, axis=0, keepdims=True) / (
                norm_gain[at : at + 1, :] * DEVICES
            )


def token_kernel(place, tokens, inv_rms, norm_gain, key_grad, *rest):
    pieces, (keys, tokens_grad, weight, sem) = rest[:8], rest[8:]
    core, y, zl = place[0], place[2], place[3]
    copies = []
    for step in range(4):
        for side in range(2):
            column = core * HALF if side == 0 else (1 - core) * HALF
            for j in range(4):
                row = (lax.rem(y + step, 4) * 4 + lax.rem(zl + j, 4)) * 128
                copies.append(
                    pltpu.make_async_copy(
                        pieces[step * 2 + side].at[j],
                        weight.at[pl.ds(pl.multiple_of(row, 128), 128), pl.ds(pl.multiple_of(column, HALF), HALF)],
                        sem.at[len(copies)],
                    )
                )
    for copy in copies:
        copy.start()
    for copy in copies:
        copy.wait()
    for rows in (slice(0, 96), slice(96, 192)):
        inv = inv_rms[rows, 0:1]
        unit = tokens[rows, :].astype(f32) * inv
        normed = (unit * norm_gain[...]).astype(bf16)
        keys[rows, :] = jnp.dot(normed, weight[...], preferred_element_type=f32).astype(bf16)
        scaled = norm_gain[...] * lax.dot_general(
            key_grad[rows, :], weight[...], (((1,), (1,)), ((), ())), preferred_element_type=f32
        )
        mean = jnp.mean(scaled * unit, axis=1, keepdims=True)
        tokens_grad[rows, :] = (inv * (scaled - unit * mean)).astype(bf16)


def call(kernel, outs, ins, args, scratch=(), flops=0, **kw):
    moved = sum(a.size * a.dtype.itemsize for a in args)
    return pl.pallas_call(
        kernel,
        out_shape=[jax.ShapeDtypeStruct(s, d) for s, d in outs],
        in_specs=ins,
        out_specs=[VMEM] * len(outs),
        scratch_shapes=list(scratch),
        compiler_params=PARAMS,
        cost_estimate=pl.CostEstimate(flops=flops, bytes_accessed=2 * moved, transcendentals=0),
    )(*args)


def local(tokens, norm_gain, weight_codes, block_scales, key_grad):
    core = lax.axis_index("core")
    place = jnp.stack(
        [core, lax.axis_index("x"), lax.axis_index("y"), lax.axis_index("zl")]
    ).astype(jnp.int32)
    gain_row = norm_gain.reshape(1, 2048)

    codes = lax.dynamic_slice_in_dim(weight_codes, core * HALF, HALF, 1)
    scales = lax.dynamic_slice_in_dim(block_scales, core * HALF, HALF, 1)
    shard = (codes.astype(f32) * scales).astype(bf16)
    normed, inv_rms, theirs = call(
        norm_kernel,
        [((192, 2048), bf16), ((192, 128), f32), ((16, 16, 2048), bf16)],
        [SMEM, HBM, HBM, HBM],
        (place, in_hbm(tokens), in_hbm(gain_row), in_hbm(key_grad)),
        scratch=[
            pltpu.VMEM((192, 2048), bf16),
            pltpu.VMEM((1, 2048), f32),
            pltpu.VMEM((192, 512), bf16),
            pltpu.SemaphoreType.DMA((3,)),
        ],
        flops=2 * 192 * 2048 * 256,
    )
    got = swap(theirs)
    (mine,) = call(
        mine_kernel,
        [((16, 16, 2048), f32)],
        [SMEM, VMEM, VMEM],
        (place, normed, key_grad),
        flops=2 * 192 * 2048 * 256,
    )
    (pair,) = call(pair_kernel, [((16, 16, 2048), bf16)], [VMEM] * 2, (mine, got))
    square = exchange(pair, ("y", "x"))

    shard_late, _ = lax.optimization_barrier((shard, pair))
    above = along_z(shard_late, lambda x, core: -1)
    across = along_z(shard_late, lambda x, core: (2, -2)[core])
    below = along_z(shard_late, lambda x, core: 1)
    stack = jnp.stack([shard, above, across, below])

    (payload,) = call(
        square_kernel,
        [((16, 16, 640), bf16)],
        [SMEM] + [VMEM] * 5,
        (place, square, shard, above, across, below),
        scratch=[pltpu.VMEM((4, 32, HALF), f32), pltpu.VMEM((4, 32, HALF), f32)],
    )
    line = exchange(payload, Z)

    stack_late, _ = lax.optimization_barrier((stack, payload))
    pieces = [stack] + [along_y(stack_late, -step) for step in range(1, 4)]
    line, *pieces = lax.optimization_barrier((line, *pieces))
    (blocks,) = call(line_kernel, [((32, 16, 640), bf16)], [VMEM], (line,))
    *late, _ = lax.optimization_barrier((*pieces, blocks))
    pieces = [part for piece, other in zip(pieces, map(swap, late)) for part in (piece, other)]
    blocks = exchange(blocks, ("y", "x", "core"))
    keys, tokens_grad = call(
        token_kernel,
        [((192, 512), bf16), ((192, 2048), bf16)],
        [SMEM, VMEM, VMEM, VMEM, VMEM] + [ANY] * 8,
        (place, tokens, inv_rms, gain_row, key_grad, *pieces),
        scratch=[pltpu.VMEM((2048, 512), bf16), pltpu.SemaphoreType.DMA((32,))],
        flops=4 * 192 * 2048 * 512,
    )
    weight_grad, gain_grad = call(
        last_kernel,
        [((128, 512), f32), ((16, 128), f32)],
        [SMEM, VMEM, VMEM],
        (place, blocks, norm_gain.reshape(16, 128)),
    )
    return keys, tokens_grad, weight_grad, gain_grad.reshape(2048)


def solution(mesh):
    fine = Mesh(mesh.devices.reshape(SIZES), AXES)
    everyone = P(AXES, None)
    group = P(("y", "zl"), None)
    in_specs = (everyone, P(), group, group, everyone)
    out_specs = (everyone, everyone, group, P())
    return jax.shard_map(local, mesh=fine, in_specs=in_specs, out_specs=out_specs, check_vma=False)
```

```python
import functools

import jax
import jax.numpy as jnp
from jax import lax
from jax.experimental import pallas as pl
from jax.experimental.pallas import tpu as pltpu
from jax.sharding import Mesh, PartitionSpec as P

eps = 1e-05
AXES = ("zh", "x", "core", "y", "zl")
SIZES = (4, 4, 2, 4, 4)
Z = ("zh", "zl")
DEVICES = 512
HALF = 256
f32, bf16 = jnp.float32, jnp.bfloat16
VMEM = pl.BlockSpec(memory_space=pltpu.VMEM)
SMEM = pl.BlockSpec(memory_space=pltpu.SMEM)
ANY = pl.BlockSpec(memory_space=pl.ANY)
HBM = pl.BlockSpec(memory_space=pltpu.HBM)
PARAMS = pltpu.CompilerParams(vmem_limit_bytes=40 * 1024 * 1024)


def in_hbm(array):
    return pltpu.with_memory_space_constraint(array, pltpu.HBM)


def exchange(blocks, axes):
    return lax.all_to_all(blocks, axes, 0, 0, tiled=False)


def swap(block):
    return lax.ppermute(block, "core", [(0, 1), (1, 0)])


def along_y(block, step):
    return lax.ppermute(block, "y", [(y, (y + step) % 4) for y in range(4)])


def along_z(block, step):
    pairs = []
    for z in range(16):
        for x in range(4):
            for core in range(2):
                to = (z + step(x, core)) % 16
                pairs.append(
                    (((z // 4 * 4 + x) * 2 + core) * 4 + z % 4, ((to // 4 * 4 + x) * 2 + core) * 4 + to % 4)
                )
    return lax.ppermute(block, ("zh", "x", "core", "zl"), pairs)


def contract_rows(a, b):
    return lax.dot_general(a, b, (((0,), (0,)), ((), ())), preferred_element_type=f32)


def put_product(normed, grad, out, dtype):
    for part_at in range(8):
        y, first = part_at // 2, part_at % 2 * 2
        part = contract_rows(normed[:, part_at * HALF : (part_at + 1) * HALF], grad).astype(dtype)
        for x in range(4):
            for k in range(4):
                row = k // 2 * 128 + x * 32 + k % 2 * 16
                column = (first * 2 + k) * HALF
                out[y * 4 + x, :, column : column + HALF] = part[row : row + 16]


def norm_kernel(place, tokens_at, gain_at, grad_at, normed, inv_rms, theirs, tokens, norm_gain, key_grad, sem):
    quarters = [slice(i * 48, i * 48 + 48) for i in range(4)]
    copies = [(gain_at, norm_gain)] + [(tokens_at.at[rows], tokens.at[rows]) for rows in quarters]
    copies = [
        pltpu.make_async_copy(source, target, sem.at[i])
        for i, (source, target) in enumerate(copies + [(grad_at, key_grad)])
    ]
    for copy in copies:
        copy.start()
    copies[0].wait()
    for copy, rows in zip(copies[1:], quarters):
        copy.wait()
        wide = tokens[rows, :].astype(f32)
        inv = lax.rsqrt(jnp.mean(wide * wide, axis=1, keepdims=True) + eps)
        inv_rms[rows, :] = jnp.broadcast_to(inv, (48, 128))
        normed[rows, :] = (wide * inv * norm_gain[...]).astype(bf16)
    copies[5].wait()
    start = pl.multiple_of((1 - place[0]) * HALF, HALF)
    put_product(normed, key_grad[:, pl.ds(start, HALF)], theirs, bf16)


def mine_kernel(place, normed, key_grad, mine):
    start = pl.multiple_of(place[0] * HALF, HALF)
    put_product(normed, key_grad[:, pl.ds(start, HALF)], mine, f32)


def pair_kernel(mine, got, out):
    for peer in range(16):
        out[peer] = (mine[peer] + got[peer].astype(f32)).astype(bf16)


def two_rows(value):
    high = value.astype(bf16).astype(f32)
    row = lax.broadcasted_iota(jnp.int32, (16, 128), 0)
    return jnp.where(row == 0, high, jnp.where(row == 1, value - high, 0.0)).astype(bf16)


def square_kernel(place, square, shard, above, across, below, out, shards, products):
    x, zl = place[1], place[3]
    for k in range(8):
        cols = slice(k * HALF, (k + 1) * HALF)
        total = square[0, :, cols].astype(f32)
        for sender in range(1, 16):
            total += square[sender, :, cols].astype(f32)
        shards[k // 2, k % 2 * 16 : k % 2 * 16 + 16] = total
    for j, piece in enumerate((shard, above, across, below)):
        which = lax.rem(zl + j, 4)
        rows = piece[pl.ds(pl.multiple_of(x * 32, 32), 32), :].astype(f32)
        products[which] = shards[which] * rows
    gain = lax.dot_general(
        jnp.ones((16, HALF), f32),
        products[...].reshape(128, HALF),
        (((1,), (1,)), ((), ())),
        preferred_element_type=f32,
        precision=lax.Precision.HIGHEST,
    )
    gains = two_rows(gain)
    for target in range(4):
        rows = shards[target].astype(bf16)
        for zh in range(4):
            z = zh * 4 + target
            out[z, :, :HALF] = rows[:16]
            out[z, :, HALF : 2 * HALF] = rows[16:]
            out[z, :, 2 * HALF :] = gains


def line_kernel(line, out):
    total = line[0].astype(f32)
    for sender in range(1, 16):
        total += line[sender].astype(f32)
    gains = two_rows(jnp.broadcast_to(total[0:1, 512:] + total[1:2, 512:], (16, 128)))
    rows = total[:, :512].astype(bf16)
    for peer in range(32):
        out[peer, :, :512] = rows
        out[peer, :, 512:] = gains


def last_kernel(place, blocks, norm_gain, weight_grad, gain_grad):
    y = place[2]
    for x in range(4):
        for core in range(2):
            block = blocks[y * 8 + x * 2 + core].astype(f32) / DEVICES
            for k in range(2):
                weight_grad[x * 32 + k * 16 : x * 32 + k * 16 + 16, core * HALF : (core + 1) * HALF] = block[
                    :, k * HALF : (k + 1) * HALF
                ]
    rows_of = []
    for peer in range(16):
        gains = blocks[peer * 2, :, 512:].astype(f32) + blocks[peer * 2 + 1, :, 512:].astype(f32)
        rows_of.append(gains[0:1] + gains[1:2])
    sums = jnp.concatenate(rows_of, axis=0)
    lane = lax.broadcasted_iota(jnp.int32, (16, 128), 1)
    peer = lax.broadcasted_iota(jnp.int32, (16, 128), 0)
    spread = (
        lax.broadcasted_iota(jnp.int32, (128, 128), 0) % 32
        == lax.broadcasted_iota(jnp.int32, (128, 128), 1) % 32
    ).astype(f32)
    stacked = jnp.concatenate([jnp.where(lane // 32 == zl, sums, 0.0) for zl in range(4)], axis=0)
    moved = lax.dot_general(
        stacked, spread, (((1,), (0,)), ((), ())), preferred_element_type=f32,
        precision=lax.Precision.HIGHEST,
    )
    for row in range(4):
        for zl in range(4):
            picked = jnp.where(peer == row * 4 + lane // 32, moved[zl * 16 : zl * 16 + 16], 0.0)
            at = row * 4 + zl
            gain_grad[at : at + 1, :] = jnp.sum(picked, axis=0, keepdims=True) / (
                norm_gain[at : at + 1, :] * DEVICES
            )


def token_kernel(place, tokens, inv_rms, norm_gain, key_grad, *rest):
    pieces, (keys, tokens_grad, weight, sem) = rest[:8], rest[8:]
    core, y, zl = place[0], place[2], place[3]
    copies = []
    for step in range(4):
        for side in range(2):
            column = core * HALF if side == 0 else (1 - core) * HALF
            for j in range(4):
                row = (lax.rem(y + step, 4) * 4 + lax.rem(zl + j, 4)) * 128
                copies.append(
                    pltpu.make_async_copy(
                        pieces[step * 2 + side].at[j],
                        weight.at[pl.ds(pl.multiple_of(row, 128), 128), pl.ds(pl.multiple_of(column, HALF), HALF)],
                        sem.at[len(copies)],
                    )
                )
    for copy in copies:
        copy.start()
    for copy in copies:
        copy.wait()
    for rows in (slice(0, 96), slice(96, 192)):
        inv = inv_rms[rows, 0:1]
        unit = tokens[rows, :].astype(f32) * inv
        normed = (unit * norm_gain[...]).astype(bf16)
        keys[rows, :] = jnp.dot(normed, weight[...], preferred_element_type=f32).astype(bf16)
        scaled = norm_gain[...] * lax.dot_general(
            key_grad[rows, :], weight[...], (((1,), (1,)), ((), ())), preferred_element_type=f32
        )
        mean = jnp.mean(scaled * unit, axis=1, keepdims=True)
        tokens_grad[rows, :] = (inv * (scaled - unit * mean)).astype(bf16)


def call(kernel, outs, ins, args, scratch=(), flops=0, **kw):
    moved = sum(a.size * a.dtype.itemsize for a in args)
    return pl.pallas_call(
        kernel,
        out_shape=[jax.ShapeDtypeStruct(s, d) for s, d in outs],
        in_specs=ins,
        out_specs=[VMEM] * len(outs),
        scratch_shapes=list(scratch),
        compiler_params=PARAMS,
        cost_estimate=pl.CostEstimate(flops=flops, bytes_accessed=2 * moved, transcendentals=0),
    )(*args)


def local(tokens, norm_gain, weight_codes, block_scales, key_grad):
    core = lax.axis_index("core")
    place = jnp.stack(
        [core, lax.axis_index("x"), lax.axis_index("y"), lax.axis_index("zl")]
    ).astype(jnp.int32)
    gain_row = norm_gain.reshape(1, 2048)

    codes = lax.dynamic_slice_in_dim(weight_codes, core * HALF, HALF, 1)
    scales = lax.dynamic_slice_in_dim(block_scales, core * HALF, HALF, 1)
    shard = (codes.astype(f32) * scales).astype(bf16)
    normed, inv_rms, theirs = call(
        norm_kernel,
        [((192, 2048), bf16), ((192, 128), f32), ((16, 16, 2048), bf16)],
        [SMEM, HBM, HBM, HBM],
        (place, in_hbm(tokens), in_hbm(gain_row), in_hbm(key_grad)),
        scratch=[
            pltpu.VMEM((192, 2048), bf16),
            pltpu.VMEM((1, 2048), f32),
            pltpu.VMEM((192, 512), bf16),
            pltpu.SemaphoreType.DMA((6,)),
        ],
        flops=2 * 192 * 2048 * 256,
    )
    got = swap(theirs)
    (mine,) = call(
        mine_kernel,
        [((16, 16, 2048), f32)],
        [SMEM, VMEM, VMEM],
        (place, normed, key_grad),
        flops=2 * 192 * 2048 * 256,
    )
    (pair,) = call(pair_kernel, [((16, 16, 2048), bf16)], [VMEM] * 2, (mine, got))
    square = exchange(pair, ("y", "x"))

    shard_late, _ = lax.optimization_barrier((shard, pair))
    above = along_z(shard_late, lambda x, core: -1)
    across = along_z(shard_late, lambda x, core: (2, -2)[core])
    below = along_z(shard_late, lambda x, core: 1)
    stack = jnp.stack([shard, above, across, below])

    (payload,) = call(
        square_kernel,
        [((16, 16, 640), bf16)],
        [SMEM] + [VMEM] * 5,
        (place, square, shard, above, across, below),
        scratch=[pltpu.VMEM((4, 32, HALF), f32), pltpu.VMEM((4, 32, HALF), f32)],
    )
    line = exchange(payload, Z)

    stack_late, _ = lax.optimization_barrier((stack, payload))
    own = stack_late
    one, two, three = (along_y(stack_late, -step) for step in (1, 2, 3))
    own_other, one_other = swap(own), swap(one)
    line, own_other, one_other, two, three = lax.optimization_barrier((line, own_other, one_other, two, three))
    (blocks,) = call(line_kernel, [((32, 16, 640), bf16)], [VMEM], (line,))
    two_late, three_late, _ = lax.optimization_barrier((two, three, blocks))
    pieces = (own, own_other, one, one_other, two, swap(two_late), three, swap(three_late))
    blocks = exchange(blocks, ("y", "x", "core"))
    keys, tokens_grad = call(
        token_kernel,
        [((192, 512), bf16), ((192, 2048), bf16)],
        [SMEM, VMEM, VMEM, VMEM, VMEM] + [ANY] * 8,
        (place, tokens, inv_rms, gain_row, key_grad, *pieces),
        scratch=[pltpu.VMEM((2048, 512), bf16), pltpu.SemaphoreType.DMA((32,))],
        flops=4 * 192 * 2048 * 512,
    )
    weight_grad, gain_grad = call(
        last_kernel,
        [((128, 512), f32), ((16, 128), f32)],
        [SMEM, VMEM, VMEM],
        (place, blocks, norm_gain.reshape(16, 128)),
    )
    return keys, tokens_grad, weight_grad, gain_grad.reshape(2048)


def solution(mesh):
    fine = Mesh(mesh.devices.reshape(SIZES), AXES)
    everyone = P(AXES, None)
    group = P(("y", "zl"), None)
    in_specs = (everyone, P(), group, group, everyone)
    out_specs = (everyone, everyone, group, P())
    return jax.shard_map(local, mesh=fine, in_specs=in_specs, out_specs=out_specs, check_vma=False)
```

```python
import functools

import jax
import jax.numpy as jnp
from jax import lax
from jax.experimental import pallas as pl
from jax.experimental.pallas import tpu as pltpu
from jax.sharding import Mesh, PartitionSpec as P

eps = 1e-05
AXES = ("zh", "x", "core", "y", "zl")
SIZES = (4, 4, 2, 4, 4)
DEVICES = 512
HALF = 256
f32, bf16 = jnp.float32, jnp.bfloat16
VMEM = pl.BlockSpec(memory_space=pltpu.VMEM)
SMEM = pl.BlockSpec(memory_space=pltpu.SMEM)
ANY = pl.BlockSpec(memory_space=pl.ANY)
HBM = pl.BlockSpec(memory_space=pltpu.HBM)
PARAMS = pltpu.CompilerParams(vmem_limit_bytes=40 * 1024 * 1024)


def in_hbm(array):
    return pltpu.with_memory_space_constraint(array, pltpu.HBM)


def exchange(blocks, axes):
    return lax.all_to_all(blocks, axes, 0, 0, tiled=False)


def swap(block):
    return lax.ppermute(block, "core", [(0, 1), (1, 0)])


def along_y(block, step):
    return lax.ppermute(block, "y", [(y, (y + step) % 4) for y in range(4)])


def along_z(block, step):
    pairs = []
    for z in range(16):
        for x in range(4):
            for core in range(2):
                to = (z + step(x, core)) % 16
                pairs.append(
                    (((z // 4 * 4 + x) * 2 + core) * 4 + z % 4, ((to // 4 * 4 + x) * 2 + core) * 4 + to % 4)
                )
    return lax.ppermute(block, ("zh", "x", "core", "zl"), pairs)


def contract_rows(a, b):
    return lax.dot_general(a, b, (((0,), (0,)), ((), ())), preferred_element_type=f32)


def put_product(normed, grad, out, dtype):
    for part_at in range(8):
        y, first = part_at // 2, part_at % 2 * 2
        part = contract_rows(normed[:, part_at * HALF : (part_at + 1) * HALF], grad).astype(dtype)
        for x in range(4):
            for k in range(4):
                row = k // 2 * 128 + x * 32 + k % 2 * 16
                column = (first * 2 + k) * HALF
                out[y * 4 + x, :, column : column + HALF] = part[row : row + 16]


def norm_kernel(place, tokens_at, gain_at, grad_at, normed, inv_rms, theirs, tokens, norm_gain, key_grad, sem):
    quarters = [slice(i * 48, i * 48 + 48) for i in range(4)]
    copies = [(gain_at, norm_gain)] + [(tokens_at.at[rows], tokens.at[rows]) for rows in quarters]
    copies = [
        pltpu.make_async_copy(source, target, sem.at[i])
        for i, (source, target) in enumerate(copies + [(grad_at, key_grad)])
    ]
    for copy in copies:
        copy.start()
    copies[0].wait()
    for copy, rows in zip(copies[1:], quarters):
        copy.wait()
        wide = tokens[rows, :].astype(f32)
        inv = lax.rsqrt(jnp.mean(wide * wide, axis=1, keepdims=True) + eps)
        inv_rms[rows, :] = jnp.broadcast_to(inv, (48, 128))
        normed[rows, :] = (wide * inv * norm_gain[...]).astype(bf16)
    copies[5].wait()
    start = pl.multiple_of((1 - place[0]) * HALF, HALF)
    put_product(normed, key_grad[:, pl.ds(start, HALF)], theirs, bf16)


def mine_kernel(place, normed, key_grad, mine):
    start = pl.multiple_of(place[0] * HALF, HALF)
    put_product(normed, key_grad[:, pl.ds(start, HALF)], mine, f32)


def pair_kernel(mine, got, out):
    for peer in range(16):
        out[peer] = (mine[peer] + got[peer].astype(f32)).astype(bf16)


def two_rows(value):
    high = value.astype(bf16).astype(f32)
    row = lax.broadcasted_iota(jnp.int32, (16, 128), 0)
    return jnp.where(row == 0, high, jnp.where(row == 1, value - high, 0.0)).astype(bf16)


def square_kernel(place, square, shard, above, across, below, out, shards, products):
    x, zl = place[1], place[3]
    for k in range(8):
        cols = slice(k * HALF, (k + 1) * HALF)
        total = square[0, :, cols].astype(f32)
        for sender in range(1, 16):
            total += square[sender, :, cols].astype(f32)
        shards[k // 2, k % 2 * 16 : k % 2 * 16 + 16] = total
    for j, piece in enumerate((shard, above, across, below)):
        which = lax.rem(zl + j, 4)
        rows = piece[pl.ds(pl.multiple_of(x * 32, 32), 32), :].astype(f32)
        products[which] = shards[which] * rows
    gain = lax.dot_general(
        jnp.ones((16, HALF), f32),
        products[...].reshape(128, HALF),
        (((1,), (1,)), ((), ())),
        preferred_element_type=f32,
        precision=lax.Precision.HIGHEST,
    )
    gains = two_rows(gain)
    for target in range(4):
        rows = shards[target].astype(bf16)
        out[target, :, :HALF] = rows[:16]
        out[target, :, HALF : 2 * HALF] = rows[16:]
        out[target, :, 2 * HALF :] = gains


def line_kernel(line, out):
    total = line[0].astype(f32)
    for sender in range(1, 4):
        total += line[sender].astype(f32)
    gains = two_rows(jnp.broadcast_to(total[0:1, 512:] + total[1:2, 512:], (16, 128)))
    rows = total[:, :512].astype(bf16)
    for peer in range(out.shape[0]):
        out[peer, :, :512] = rows
        out[peer, :, 512:] = gains


def last_kernel(place, blocks, norm_gain, weight_grad, gain_grad):
    y = place[2]
    for x in range(4):
        for core in range(2):
            block = blocks[y * 8 + x * 2 + core].astype(f32) / DEVICES
            for k in range(2):
                weight_grad[x * 32 + k * 16 : x * 32 + k * 16 + 16, core * HALF : (core + 1) * HALF] = block[
                    :, k * HALF : (k + 1) * HALF
                ]
    rows_of = []
    for peer in range(16):
        gains = blocks[peer * 2, :, 512:].astype(f32) + blocks[peer * 2 + 1, :, 512:].astype(f32)
        rows_of.append(gains[0:1] + gains[1:2])
    sums = jnp.concatenate(rows_of, axis=0)
    lane = lax.broadcasted_iota(jnp.int32, (16, 128), 1)
    peer = lax.broadcasted_iota(jnp.int32, (16, 128), 0)
    spread = (
        lax.broadcasted_iota(jnp.int32, (128, 128), 0) % 32
        == lax.broadcasted_iota(jnp.int32, (128, 128), 1) % 32
    ).astype(f32)
    stacked = jnp.concatenate([jnp.where(lane // 32 == zl, sums, 0.0) for zl in range(4)], axis=0)
    moved = lax.dot_general(
        stacked, spread, (((1,), (0,)), ((), ())), preferred_element_type=f32,
        precision=lax.Precision.HIGHEST,
    )
    for row in range(4):
        for zl in range(4):
            picked = jnp.where(peer == row * 4 + lane // 32, moved[zl * 16 : zl * 16 + 16], 0.0)
            at = row * 4 + zl
            gain_grad[at : at + 1, :] = jnp.sum(picked, axis=0, keepdims=True) / (
                norm_gain[at : at + 1, :] * DEVICES
            )


def token_kernel(place, tokens, inv_rms, norm_gain, key_grad, *rest):
    pieces, (keys, tokens_grad, weight, sem) = rest[:4], rest[4:]
    core, y, zl = place[0], place[2], place[3]
    copies = []
    for step in range(4):
        for side in range(2):
            column = core * HALF if side == 0 else (1 - core) * HALF
            for j in range(4):
                row = (lax.rem(y + step, 4) * 4 + lax.rem(zl + j, 4)) * 128
                copies.append(
                    pltpu.make_async_copy(
                        pieces[side * 2 + step // 2].at[step % 2 * 4 + j],
                        weight.at[pl.ds(pl.multiple_of(row, 128), 128), pl.ds(pl.multiple_of(column, HALF), HALF)],
                        sem.at[len(copies)],
                    )
                )
    for copy in copies:
        copy.start()
    for copy in copies:
        copy.wait()
    for rows in (slice(0, 96), slice(96, 192)):
        inv = inv_rms[rows, 0:1]
        unit = tokens[rows, :].astype(f32) * inv
        normed = (unit * norm_gain[...]).astype(bf16)
        keys[rows, :] = jnp.dot(normed, weight[...], preferred_element_type=f32).astype(bf16)
        scaled = norm_gain[...] * lax.dot_general(
            key_grad[rows, :], weight[...], (((1,), (1,)), ((), ())), preferred_element_type=f32
        )
        mean = jnp.mean(scaled * unit, axis=1, keepdims=True)
        tokens_grad[rows, :] = (inv * (scaled - unit * mean)).astype(bf16)


def call(kernel, outs, ins, args, scratch=(), flops=0, **kw):
    moved = sum(a.size * a.dtype.itemsize for a in args)
    return pl.pallas_call(
        kernel,
        out_shape=[jax.ShapeDtypeStruct(s, d) for s, d in outs],
        in_specs=ins,
        out_specs=[VMEM] * len(outs),
        scratch_shapes=list(scratch),
        compiler_params=PARAMS,
        cost_estimate=pl.CostEstimate(flops=flops, bytes_accessed=2 * moved, transcendentals=0),
    )(*args)


def local(tokens, norm_gain, weight_codes, block_scales, key_grad):
    core = lax.axis_index("core")
    place = jnp.stack(
        [core, lax.axis_index("x"), lax.axis_index("y"), lax.axis_index("zl")]
    ).astype(jnp.int32)
    gain_row = norm_gain.reshape(1, 2048)

    codes = lax.dynamic_slice_in_dim(weight_codes, core * HALF, HALF, 1)
    scales = lax.dynamic_slice_in_dim(block_scales, core * HALF, HALF, 1)
    shard = (codes.astype(f32) * scales).astype(bf16)
    normed, inv_rms, theirs = call(
        norm_kernel,
        [((192, 2048), bf16), ((192, 128), f32), ((16, 16, 2048), bf16)],
        [SMEM, HBM, HBM, HBM],
        (place, in_hbm(tokens), in_hbm(gain_row), in_hbm(key_grad)),
        scratch=[
            pltpu.VMEM((192, 2048), bf16),
            pltpu.VMEM((1, 2048), f32),
            pltpu.VMEM((192, 512), bf16),
            pltpu.SemaphoreType.DMA((6,)),
        ],
        flops=2 * 192 * 2048 * 256,
    )
    got = swap(theirs)
    (mine,) = call(
        mine_kernel,
        [((16, 16, 2048), f32)],
        [SMEM, VMEM, VMEM],
        (place, normed, key_grad),
        flops=2 * 192 * 2048 * 256,
    )
    (pair,) = call(pair_kernel, [((16, 16, 2048), bf16)], [VMEM] * 2, (mine, got))
    square = exchange(pair, ("y", "x"))

    shard_late, _ = lax.optimization_barrier((shard, pair))
    above = along_z(shard_late, lambda x, core: -1)
    across = along_z(shard_late, lambda x, core: (2, -2)[core])
    below = along_z(shard_late, lambda x, core: 1)
    stack = jnp.stack([shard, above, across, below])

    (payload,) = call(
        square_kernel,
        [((4, 16, 640), bf16)],
        [SMEM] + [VMEM] * 5,
        (place, square, shard, above, across, below),
        scratch=[pltpu.VMEM((4, 32, HALF), f32), pltpu.VMEM((4, 32, HALF), f32)],
    )
    near = exchange(payload, "zl")
    stack_late, _ = lax.optimization_barrier((stack, payload))
    one, two, three = (along_y(stack_late, -step) for step in (1, 2, 3))
    (near_sum,) = call(line_kernel, [((4, 16, 640), bf16)], [VMEM], (near,))
    far = exchange(near_sum, "zh")
    halves = jnp.concatenate([stack, one], axis=0), jnp.concatenate([two, three], axis=0)
    far, *halves = lax.optimization_barrier((far, *halves))
    (blocks,) = call(line_kernel, [((32, 16, 640), bf16)], [VMEM], (far,))
    *halves_late, _ = lax.optimization_barrier((*halves, blocks))
    pieces = (*halves, *map(swap, halves_late))
    blocks = exchange(blocks, ("y", "x", "core"))
    keys, tokens_grad = call(
        token_kernel,
        [((192, 512), bf16), ((192, 2048), bf16)],
        [SMEM, VMEM, VMEM, VMEM, VMEM] + [ANY] * 4,
        (place, tokens, inv_rms, gain_row, key_grad, *pieces),
        scratch=[pltpu.VMEM((2048, 512), bf16), pltpu.SemaphoreType.DMA((32,))],
        flops=4 * 192 * 2048 * 512,
    )
    blocks, keys, tokens_grad = lax.optimization_barrier((blocks, keys, tokens_grad))
    weight_grad, gain_grad = call(
        last_kernel,
        [((128, 512), f32), ((16, 128), f32)],
        [SMEM, VMEM, VMEM],
        (place, blocks, norm_gain.reshape(16, 128)),
    )
    return keys, tokens_grad, weight_grad, gain_grad.reshape(2048)


def solution(mesh):
    fine = Mesh(mesh.devices.reshape(SIZES), AXES)
    everyone = P(AXES, None)
    group = P(("y", "zl"), None)
    in_specs = (everyone, P(), group, group, everyone)
    out_specs = (everyone, everyone, group, P())
    return jax.shard_map(local, mesh=fine, in_specs=in_specs, out_specs=out_specs, check_vma=False)
```

```python
import functools

import jax
import jax.numpy as jnp
from jax import lax
from jax.experimental import pallas as pl
from jax.experimental.pallas import tpu as pltpu
from jax.sharding import Mesh, PartitionSpec as P

eps = 1e-05
AXES = ("zh", "x", "core", "y", "zl")
SIZES = (4, 4, 2, 4, 4)
DEVICES = 512
HALF = 256
f32, bf16 = jnp.float32, jnp.bfloat16
VMEM = pl.BlockSpec(memory_space=pltpu.VMEM)
SMEM = pl.BlockSpec(memory_space=pltpu.SMEM)
ANY = pl.BlockSpec(memory_space=pl.ANY)
HBM = pl.BlockSpec(memory_space=pltpu.HBM)
PARAMS = pltpu.CompilerParams(vmem_limit_bytes=40 * 1024 * 1024)


def in_hbm(array):
    return pltpu.with_memory_space_constraint(array, pltpu.HBM)


def exchange(blocks, axes):
    return lax.all_to_all(blocks, axes, 0, 0, tiled=False)


def swap(block):
    return lax.ppermute(block, "core", [(0, 1), (1, 0)])


def along_y(block, step):
    return lax.ppermute(block, "y", [(y, (y + step) % 4) for y in range(4)])


def along_z(block, step):
    pairs = []
    for z in range(16):
        for x in range(4):
            for core in range(2):
                to = (z + step(x, core)) % 16
                pairs.append(
                    (((z // 4 * 4 + x) * 2 + core) * 4 + z % 4, ((to // 4 * 4 + x) * 2 + core) * 4 + to % 4)
                )
    return lax.ppermute(block, ("zh", "x", "core", "zl"), pairs)


def contract_rows(a, b):
    return lax.dot_general(a, b, (((0,), (0,)), ((), ())), preferred_element_type=f32)


def put_product(normed, grad, out, dtype):
    for part_at in range(8):
        y, first = part_at // 2, part_at % 2 * 2
        part = contract_rows(normed[:, part_at * HALF : (part_at + 1) * HALF], grad).astype(dtype)
        for x in range(4):
            for k in range(4):
                row = k // 2 * 128 + x * 32 + k % 2 * 16
                column = (first * 2 + k) * HALF
                out[y * 4 + x, :, column : column + HALF] = part[row : row + 16]


def norm_kernel(place, tokens_at, gain_at, grad_at, normed, inv_rms, theirs, tokens, norm_gain, key_grad, sem):
    quarters = [slice(i * 48, i * 48 + 48) for i in range(4)]
    copies = [(gain_at, norm_gain)] + [(tokens_at.at[rows], tokens.at[rows]) for rows in quarters]
    copies = [
        pltpu.make_async_copy(source, target, sem.at[i])
        for i, (source, target) in enumerate(copies + [(grad_at, key_grad)])
    ]
    for copy in copies:
        copy.start()
    copies[0].wait()
    for copy, rows in zip(copies[1:], quarters):
        copy.wait()
        wide = tokens[rows, :].astype(f32)
        inv = lax.rsqrt(jnp.mean(wide * wide, axis=1, keepdims=True) + eps)
        inv_rms[rows, :] = jnp.broadcast_to(inv, (48, 128))
        normed[rows, :] = (wide * inv * norm_gain[...]).astype(bf16)
    copies[5].wait()
    start = pl.multiple_of((1 - place[0]) * HALF, HALF)
    put_product(normed, key_grad[:, pl.ds(start, HALF)], theirs, bf16)


def mine_kernel(place, normed, key_grad, mine):
    start = pl.multiple_of(place[0] * HALF, HALF)
    put_product(normed, key_grad[:, pl.ds(start, HALF)], mine, f32)


def pair_kernel(mine, got, out):
    for peer in range(16):
        out[peer] = (mine[peer] + got[peer].astype(f32)).astype(bf16)


def two_rows(value):
    high = value.astype(bf16).astype(f32)
    row = lax.broadcasted_iota(jnp.int32, (16, 128), 0)
    return jnp.where(row == 0, high, jnp.where(row == 1, value - high, 0.0)).astype(bf16)


def square_kernel(place, square, shard, above, across, below, out, shards, products):
    x, zl = place[1], place[3]
    for k in range(8):
        cols = slice(k * HALF, (k + 1) * HALF)
        total = square[0, :, cols].astype(f32)
        for sender in range(1, 16):
            total += square[sender, :, cols].astype(f32)
        shards[k // 2, k % 2 * 16 : k % 2 * 16 + 16] = total
    for j, piece in enumerate((shard, above, across, below)):
        which = lax.rem(zl + j, 4)
        rows = piece[pl.ds(pl.multiple_of(x * 32, 32), 32), :].astype(f32)
        products[which] = shards[which] * rows
    gain = lax.dot_general(
        jnp.ones((16, HALF), f32),
        products[...].reshape(128, HALF),
        (((1,), (1,)), ((), ())),
        preferred_element_type=f32,
        precision=lax.Precision.HIGHEST,
    )
    gains = two_rows(gain)
    for target in range(4):
        rows = shards[target].astype(bf16)
        for zh in range(4):
            z = zh * 4 + target
            out[z, :, :HALF] = rows[:16]
            out[z, :, HALF : 2 * HALF] = rows[16:]
            out[z, :, 2 * HALF :] = gains


def line_kernel(line, out):
    total = line[0].astype(f32)
    for sender in range(1, 16):
        total += line[sender].astype(f32)
    gains = two_rows(jnp.broadcast_to(total[0:1, 512:] + total[1:2, 512:], (16, 128)))
    rows = total[:, :512].astype(bf16)
    for peer in range(out.shape[0]):
        out[peer, :, :512] = rows
        out[peer, :, 512:] = gains


def last_kernel(place, blocks, norm_gain, weight_grad, gain_grad):
    y = place[2]
    for x in range(4):
        for core in range(2):
            block = blocks[y * 8 + x * 2 + core].astype(f32) / DEVICES
            for k in range(2):
                weight_grad[x * 32 + k * 16 : x * 32 + k * 16 + 16, core * HALF : (core + 1) * HALF] = block[
                    :, k * HALF : (k + 1) * HALF
                ]
    rows_of = []
    for peer in range(16):
        gains = blocks[peer * 2, :, 512:].astype(f32) + blocks[peer * 2 + 1, :, 512:].astype(f32)
        rows_of.append(gains[0:1] + gains[1:2])
    sums = jnp.concatenate(rows_of, axis=0)
    lane = lax.broadcasted_iota(jnp.int32, (16, 128), 1)
    peer = lax.broadcasted_iota(jnp.int32, (16, 128), 0)
    spread = (
        lax.broadcasted_iota(jnp.int32, (128, 128), 0) % 32
        == lax.broadcasted_iota(jnp.int32, (128, 128), 1) % 32
    ).astype(f32)
    stacked = jnp.concatenate([jnp.where(lane // 32 == zl, sums, 0.0) for zl in range(4)], axis=0)
    moved = lax.dot_general(
        stacked, spread, (((1,), (0,)), ((), ())), preferred_element_type=f32,
        precision=lax.Precision.HIGHEST,
    )
    for row in range(4):
        for zl in range(4):
            picked = jnp.where(peer == row * 4 + lane // 32, moved[zl * 16 : zl * 16 + 16], 0.0)
            at = row * 4 + zl
            gain_grad[at : at + 1, :] = jnp.sum(picked, axis=0, keepdims=True) / (
                norm_gain[at : at + 1, :] * DEVICES
            )


def token_kernel(place, tokens, inv_rms, norm_gain, key_grad, *rest):
    pieces, (keys, tokens_grad, weight, sem) = rest[:4], rest[4:]
    core, y, zl = place[0], place[2], place[3]
    copies = []
    for step in range(4):
        for side in range(2):
            column = core * HALF if side == 0 else (1 - core) * HALF
            for j in range(4):
                row = (lax.rem(y + step, 4) * 4 + lax.rem(zl + j, 4)) * 128
                copies.append(
                    pltpu.make_async_copy(
                        pieces[side * 2 + step // 2].at[step % 2 * 4 + j],
                        weight.at[pl.ds(pl.multiple_of(row, 128), 128), pl.ds(pl.multiple_of(column, HALF), HALF)],
                        sem.at[len(copies)],
                    )
                )
    for copy in copies:
        copy.start()
    for copy in copies:
        copy.wait()
    for rows in (slice(0, 96), slice(96, 192)):
        inv = inv_rms[rows, 0:1]
        unit = tokens[rows, :].astype(f32) * inv
        normed = (unit * norm_gain[...]).astype(bf16)
        keys[rows, :] = jnp.dot(normed, weight[...], preferred_element_type=f32).astype(bf16)
        scaled = norm_gain[...] * lax.dot_general(
            key_grad[rows, :], weight[...], (((1,), (1,)), ((), ())), preferred_element_type=f32
        )
        mean = jnp.mean(scaled * unit, axis=1, keepdims=True)
        tokens_grad[rows, :] = (inv * (scaled - unit * mean)).astype(bf16)


def call(kernel, outs, ins, args, scratch=(), flops=0, **kw):
    moved = sum(a.size * a.dtype.itemsize for a in args)
    return pl.pallas_call(
        kernel,
        out_shape=[jax.ShapeDtypeStruct(s, d) for s, d in outs],
        in_specs=ins,
        out_specs=[VMEM] * len(outs),
        scratch_shapes=list(scratch),
        compiler_params=PARAMS,
        cost_estimate=pl.CostEstimate(flops=flops, bytes_accessed=2 * moved, transcendentals=0),
    )(*args)


def local(tokens, norm_gain, weight_codes, block_scales, key_grad):
    core = lax.axis_index("core")
    place = jnp.stack(
        [core, lax.axis_index("x"), lax.axis_index("y"), lax.axis_index("zl")]
    ).astype(jnp.int32)
    gain_row = norm_gain.reshape(1, 2048)

    codes = lax.dynamic_slice_in_dim(weight_codes, core * HALF, HALF, 1)
    scales = lax.dynamic_slice_in_dim(block_scales, core * HALF, HALF, 1)
    shard = (codes.astype(f32) * scales).astype(bf16)
    normed, inv_rms, theirs = call(
        norm_kernel,
        [((192, 2048), bf16), ((192, 128), f32), ((16, 16, 2048), bf16)],
        [SMEM, HBM, HBM, HBM],
        (place, in_hbm(tokens), in_hbm(gain_row), in_hbm(key_grad)),
        scratch=[
            pltpu.VMEM((192, 2048), bf16),
            pltpu.VMEM((1, 2048), f32),
            pltpu.VMEM((192, 512), bf16),
            pltpu.SemaphoreType.DMA((6,)),
        ],
        flops=2 * 192 * 2048 * 256,
    )
    got = swap(theirs)
    (mine,) = call(
        mine_kernel,
        [((16, 16, 2048), f32)],
        [SMEM, VMEM, VMEM],
        (place, normed, key_grad),
        flops=2 * 192 * 2048 * 256,
    )
    (pair,) = call(pair_kernel, [((16, 16, 2048), bf16)], [VMEM] * 2, (mine, got))
    square = exchange(pair, ("y", "x"))

    shard_late, _ = lax.optimization_barrier((shard, pair))
    above = along_z(shard_late, lambda x, core: -1)
    across = along_z(shard_late, lambda x, core: (2, -2)[core])
    below = along_z(shard_late, lambda x, core: 1)
    stack = jnp.stack([shard, above, across, below])

    (payload,) = call(
        square_kernel,
        [((16, 16, 640), bf16)],
        [SMEM] + [VMEM] * 5,
        (place, square, shard, above, across, below),
        scratch=[pltpu.VMEM((4, 32, HALF), f32), pltpu.VMEM((4, 32, HALF), f32)],
    )
    line = exchange(payload, ("zh", "zl"))
    stack_late, _ = lax.optimization_barrier((stack, payload))
    one, two, three = (along_y(stack_late, -step) for step in (1, 2, 3))
    halves = jnp.concatenate([stack, one], axis=0), jnp.concatenate([two, three], axis=0)
    line, *halves = lax.optimization_barrier((line, *halves))
    (blocks,) = call(line_kernel, [((32, 16, 640), bf16)], [VMEM], (line,))
    *halves_late, _ = lax.optimization_barrier((*halves, blocks))
    pieces = (*halves, *map(swap, halves_late))
    blocks = exchange(blocks, ("y", "x", "core"))
    keys, tokens_grad = call(
        token_kernel,
        [((192, 512), bf16), ((192, 2048), bf16)],
        [SMEM, VMEM, VMEM, VMEM, VMEM] + [ANY] * 4,
        (place, tokens, inv_rms, gain_row, key_grad, *pieces),
        scratch=[pltpu.VMEM((2048, 512), bf16), pltpu.SemaphoreType.DMA((32,))],
        flops=4 * 192 * 2048 * 512,
    )
    blocks, keys, tokens_grad = lax.optimization_barrier((blocks, keys, tokens_grad))
    weight_grad, gain_grad = call(
        last_kernel,
        [((128, 512), f32), ((16, 128), f32)],
        [SMEM, VMEM, VMEM],
        (place, blocks, norm_gain.reshape(16, 128)),
    )
    return keys, tokens_grad, weight_grad, gain_grad.reshape(2048)


def solution(mesh):
    fine = Mesh(mesh.devices.reshape(SIZES), AXES)
    everyone = P(AXES, None)
    group = P(("y", "zl"), None)
    in_specs = (everyone, P(), group, group, everyone)
    out_specs = (everyone, everyone, group, P())
    return jax.shard_map(local, mesh=fine, in_specs=in_specs, out_specs=out_specs, check_vma=False)
```

```python
import functools

import jax
import jax.numpy as jnp
from jax import lax
from jax.experimental import pallas as pl
from jax.experimental.pallas import tpu as pltpu
from jax.sharding import Mesh, PartitionSpec as P

eps = 1e-05
AXES = ("zh", "x", "core", "y", "zl")
SIZES = (4, 4, 2, 4, 4)
DEVICES = 512
HALF = 256
f32, bf16 = jnp.float32, jnp.bfloat16
VMEM = pl.BlockSpec(memory_space=pltpu.VMEM)
SMEM = pl.BlockSpec(memory_space=pltpu.SMEM)
ANY = pl.BlockSpec(memory_space=pl.ANY)
HBM = pl.BlockSpec(memory_space=pltpu.HBM)
PARAMS = pltpu.CompilerParams(vmem_limit_bytes=40 * 1024 * 1024)


def in_hbm(array):
    return pltpu.with_memory_space_constraint(array, pltpu.HBM)


def exchange(blocks, axes):
    return lax.all_to_all(blocks, axes, 0, 0, tiled=False)


def swap(block):
    return lax.ppermute(block, "core", [(0, 1), (1, 0)])


def along_y(block, step):
    return lax.ppermute(block, "y", [(y, (y + step) % 4) for y in range(4)])


def along_z(block, step):
    pairs = []
    for z in range(16):
        for x in range(4):
            for core in range(2):
                to = (z + step(x, core)) % 16
                pairs.append(
                    (((z // 4 * 4 + x) * 2 + core) * 4 + z % 4, ((to // 4 * 4 + x) * 2 + core) * 4 + to % 4)
                )
    return lax.ppermute(block, ("zh", "x", "core", "zl"), pairs)


def contract_rows(a, b):
    return lax.dot_general(a, b, (((0,), (0,)), ((), ())), preferred_element_type=f32)


def put_product(normed, grad, out, dtype):
    for part_at in range(8):
        y, first = part_at // 2, part_at % 2 * 2
        part = contract_rows(normed[:, part_at * HALF : (part_at + 1) * HALF], grad).astype(dtype)
        for x in range(4):
            for k in range(4):
                row = k // 2 * 128 + x * 32 + k % 2 * 16
                column = (first * 2 + k) * HALF
                out[y * 4 + x, :, column : column + HALF] = part[row : row + 16]


def norm_kernel(place, tokens_at, gain_at, grad_at, normed, inv_rms, theirs, tokens, norm_gain, key_grad, sem):
    quarters = [slice(i * 48, i * 48 + 48) for i in range(4)]
    copies = [(gain_at, norm_gain)] + [(tokens_at.at[rows], tokens.at[rows]) for rows in quarters]
    copies = [
        pltpu.make_async_copy(source, target, sem.at[i])
        for i, (source, target) in enumerate(copies + [(grad_at, key_grad)])
    ]
    for copy in copies:
        copy.start()
    copies[0].wait()
    for copy, rows in zip(copies[1:], quarters):
        copy.wait()
        wide = tokens[rows, :].astype(f32)
        inv = lax.rsqrt(jnp.mean(wide * wide, axis=1, keepdims=True) + eps)
        inv_rms[rows, :] = jnp.broadcast_to(inv, (48, 128))
        normed[rows, :] = (wide * inv * norm_gain[...]).astype(bf16)
    copies[5].wait()
    start = pl.multiple_of((1 - place[0]) * HALF, HALF)
    put_product(normed, key_grad[:, pl.ds(start, HALF)], theirs, bf16)


def mine_kernel(place, normed, key_grad, mine):
    start = pl.multiple_of(place[0] * HALF, HALF)
    put_product(normed, key_grad[:, pl.ds(start, HALF)], mine, f32)


def copy_out(pairs, sem):
    copies = [pltpu.make_async_copy(source, target, sem.at[i]) for i, (source, target) in enumerate(pairs)]
    for copy in copies:
        copy.start()
    return copies


def pair_kernel(mine, got, out, held, sem):
    copies = []
    for part in range(4):
        peers = slice(part * 4, part * 4 + 4)
        for peer in range(part * 4, part * 4 + 4):
            held[peer] = (mine[peer] + got[peer].astype(f32)).astype(bf16)
        copies += copy_out([(held.at[peers], out.at[peers])], sem.at[pl.ds(part, 1)])
    for copy in copies:
        copy.wait()


def two_rows(value):
    high = value.astype(bf16).astype(f32)
    row = lax.broadcasted_iota(jnp.int32, (8, 128), 0)
    return jnp.where(row == 0, high, jnp.where(row == 1, value - high, 0.0)).astype(bf16)


def square_kernel(place, square, shard, above, across, below, out, shards, products, held, sem):
    x, zl = place[1], place[3]
    for k in range(8):
        cols = slice(k * HALF, (k + 1) * HALF)
        total = square[0, :, cols].astype(f32)
        for sender in range(1, 16):
            total += square[sender, :, cols].astype(f32)
        shards[k // 2, k % 2 * 16 : k % 2 * 16 + 16] = total
    for j, piece in enumerate((shard, above, across, below)):
        which = lax.rem(zl + j, 4)
        rows = piece[pl.ds(pl.multiple_of(x * 32, 32), 32), :].astype(f32)
        products[which] = shards[which] * rows
    gain = lax.dot_general(
        jnp.ones((8, HALF), f32),
        products[...].reshape(128, HALF),
        (((1,), (1,)), ((), ())),
        preferred_element_type=f32,
        precision=lax.Precision.HIGHEST,
    )
    gains = two_rows(gain)
    for target in range(4):
        for k in range(4):
            held[target, :, k * HALF : (k + 1) * HALF] = shards[target, k * 8 : k * 8 + 8].astype(bf16)
        held[target, :, 4 * HALF :] = gains
    for copy in copy_out([(held, out.at[zh * 4 : zh * 4 + 4]) for zh in range(4)], sem):
        copy.wait()


def line_kernel(line, out, held, sem):
    total = line[0].astype(f32)
    for sender in range(1, 16):
        total += line[sender].astype(f32)
    gains = two_rows(jnp.broadcast_to(total[0:1, 4 * HALF :] + total[1:2, 4 * HALF :], (8, 128)))
    rows = total[:, : 4 * HALF].astype(bf16)
    for peer in range(8):
        held[peer, :, : 4 * HALF] = rows
        held[peer, :, 4 * HALF :] = gains
    for copy in copy_out([(held, out.at[y * 8 : y * 8 + 8]) for y in range(4)], sem):
        copy.wait()


def last_kernel(place, blocks, norm_gain, weight_grad, gain_grad):
    y = place[2]
    for x in range(4):
        for core in range(2):
            block = blocks[y * 8 + x * 2 + core].astype(f32) / DEVICES
            for k in range(4):
                at = x * 32 + k * 8
                weight_grad[at : at + 8, core * HALF : (core + 1) * HALF] = block[:, k * HALF : (k + 1) * HALF]
    rows_of = []
    for peer in range(16):
        gains = blocks[peer * 2, :, 4 * HALF :].astype(f32) + blocks[peer * 2 + 1, :, 4 * HALF :].astype(f32)
        rows_of.append(gains[0:1] + gains[1:2])
    sums = jnp.concatenate(rows_of, axis=0)
    lane = lax.broadcasted_iota(jnp.int32, (16, 128), 1)
    peer = lax.broadcasted_iota(jnp.int32, (16, 128), 0)
    spread = (
        lax.broadcasted_iota(jnp.int32, (128, 128), 0) % 32
        == lax.broadcasted_iota(jnp.int32, (128, 128), 1) % 32
    ).astype(f32)
    stacked = jnp.concatenate([jnp.where(lane // 32 == zl, sums, 0.0) for zl in range(4)], axis=0)
    moved = lax.dot_general(
        stacked, spread, (((1,), (0,)), ((), ())), preferred_element_type=f32,
        precision=lax.Precision.HIGHEST,
    )
    for row in range(4):
        for zl in range(4):
            picked = jnp.where(peer == row * 4 + lane // 32, moved[zl * 16 : zl * 16 + 16], 0.0)
            at = row * 4 + zl
            gain_grad[at : at + 1, :] = jnp.sum(picked, axis=0, keepdims=True) / (
                norm_gain[at : at + 1, :] * DEVICES
            )


def token_kernel(place, tokens, inv_rms, norm_gain, key_grad, *rest):
    pieces, (keys, tokens_grad, weight, sem) = rest[:4], rest[4:]
    core, y, zl = place[0], place[2], place[3]
    copies = []
    for step in range(4):
        for side in range(2):
            column = core * HALF if side == 0 else (1 - core) * HALF
            for j in range(4):
                row = (lax.rem(y + step, 4) * 4 + lax.rem(zl + j, 4)) * 128
                copies.append(
                    pltpu.make_async_copy(
                        pieces[side * 2 + step // 2].at[step % 2 * 4 + j],
                        weight.at[pl.ds(pl.multiple_of(row, 128), 128), pl.ds(pl.multiple_of(column, HALF), HALF)],
                        sem.at[len(copies)],
                    )
                )
    for copy in copies:
        copy.start()
    for copy in copies:
        copy.wait()
    for rows in (slice(0, 96), slice(96, 192)):
        inv = inv_rms[rows, 0:1]
        unit = tokens[rows, :].astype(f32) * inv
        normed = (unit * norm_gain[...]).astype(bf16)
        keys[rows, :] = jnp.dot(normed, weight[...], preferred_element_type=f32).astype(bf16)
        scaled = norm_gain[...] * lax.dot_general(
            key_grad[rows, :], weight[...], (((1,), (1,)), ((), ())), preferred_element_type=f32
        )
        mean = jnp.mean(scaled * unit, axis=1, keepdims=True)
        tokens_grad[rows, :] = (inv * (scaled - unit * mean)).astype(bf16)


def call(kernel, outs, ins, args, scratch=(), flops=0, out_specs=None):
    moved = sum(a.size * a.dtype.itemsize for a in args)
    return pl.pallas_call(
        kernel,
        out_shape=[jax.ShapeDtypeStruct(s, d) for s, d in outs],
        in_specs=ins,
        out_specs=out_specs or [VMEM] * len(outs),
        scratch_shapes=list(scratch),
        compiler_params=PARAMS,
        cost_estimate=pl.CostEstimate(flops=flops, bytes_accessed=2 * moved, transcendentals=0),
    )(*args)


def local(tokens, norm_gain, weight_codes, block_scales, key_grad):
    core = lax.axis_index("core")
    place = jnp.stack(
        [core, lax.axis_index("x"), lax.axis_index("y"), lax.axis_index("zl")]
    ).astype(jnp.int32)
    gain_row = norm_gain.reshape(1, 2048)

    codes = lax.dynamic_slice_in_dim(weight_codes, core * HALF, HALF, 1)
    scales = lax.dynamic_slice_in_dim(block_scales, core * HALF, HALF, 1)
    shard = (codes.astype(f32) * scales).astype(bf16)
    normed, inv_rms, theirs = call(
        norm_kernel,
        [((192, 2048), bf16), ((192, 128), f32), ((16, 16, 2048), bf16)],
        [SMEM, HBM, HBM, HBM],
        (place, in_hbm(tokens), in_hbm(gain_row), in_hbm(key_grad)),
        scratch=[
            pltpu.VMEM((192, 2048), bf16),
            pltpu.VMEM((1, 2048), f32),
            pltpu.VMEM((192, 512), bf16),
            pltpu.SemaphoreType.DMA((6,)),
        ],
        flops=2 * 192 * 2048 * 256,
    )
    got = swap(theirs)
    (mine,) = call(
        mine_kernel,
        [((16, 16, 2048), f32)],
        [SMEM, VMEM, VMEM],
        (place, normed, key_grad),
        flops=2 * 192 * 2048 * 256,
    )
    (pair,) = call(pair_kernel, [((16, 16, 2048), bf16)], [VMEM] * 2, (mine, got), scratch=[pltpu.VMEM((16, 16, 2048), bf16), pltpu.SemaphoreType.DMA((4,))], out_specs=[ANY])
    square = exchange(pair, ("y", "x"))

    shard_late, _ = lax.optimization_barrier((shard, pair))
    above = along_z(shard_late, lambda x, core: -1)
    across = along_z(shard_late, lambda x, core: (2, -2)[core])
    below = along_z(shard_late, lambda x, core: 1)
    stack = jnp.stack([shard, above, across, below])

    (payload,) = call(
        square_kernel,
        [((16, 8, 1152), bf16)],
        [SMEM] + [VMEM] * 5,
        (place, square, shard, above, across, below),
        scratch=[
            pltpu.VMEM((4, 32, HALF), f32),
            pltpu.VMEM((4, 32, HALF), f32),
            pltpu.VMEM((4, 8, 1152), bf16),
            pltpu.SemaphoreType.DMA((4,)),
        ],
        out_specs=[ANY],
    )
    line = exchange(payload, ("zh", "zl"))
    stack_late, _ = lax.optimization_barrier((stack, payload))
    one, two, three = (along_y(stack_late, -step) for step in (1, 2, 3))
    halves = jnp.concatenate([stack, one], axis=0), jnp.concatenate([two, three], axis=0)
    line, *halves = lax.optimization_barrier((line, *halves))
    (blocks,) = call(
        line_kernel,
        [((32, 8, 1152), bf16)],
        [VMEM],
        (line,),
        scratch=[pltpu.VMEM((8, 8, 1152), bf16), pltpu.SemaphoreType.DMA((4,))],
        out_specs=[ANY],
    )
    *halves_late, _ = lax.optimization_barrier((*halves, blocks))
    pieces = (*halves, *map(swap, halves_late))
    blocks = exchange(blocks, ("y", "x", "core"))
    keys, tokens_grad = call(
        token_kernel,
        [((192, 512), bf16), ((192, 2048), bf16)],
        [SMEM, VMEM, VMEM, VMEM, VMEM] + [ANY] * 4,
        (place, tokens, inv_rms, gain_row, key_grad, *pieces),
        scratch=[pltpu.VMEM((2048, 512), bf16), pltpu.SemaphoreType.DMA((32,))],
        flops=4 * 192 * 2048 * 512,
    )
    blocks, keys, tokens_grad = lax.optimization_barrier((blocks, keys, tokens_grad))
    weight_grad, gain_grad = call(
        last_kernel,
        [((128, 512), f32), ((16, 128), f32)],
        [SMEM, VMEM, VMEM],
        (place, blocks, norm_gain.reshape(16, 128)),
    )
    return keys, tokens_grad, weight_grad, gain_grad.reshape(2048)


def solution(mesh):
    fine = Mesh(mesh.devices.reshape(SIZES), AXES)
    everyone = P(AXES, None)
    group = P(("y", "zl"), None)
    in_specs = (everyone, P(), group, group, everyone)
    out_specs = (everyone, everyone, group, P())
    return jax.shard_map(local, mesh=fine, in_specs=in_specs, out_specs=out_specs, check_vma=False)
```

```python
import functools

import jax
import jax.numpy as jnp
from jax import lax
from jax.experimental import pallas as pl
from jax.experimental.pallas import tpu as pltpu
from jax.sharding import Mesh, PartitionSpec as P

eps = 1e-05
AXES = ("zh", "x", "core", "y", "zl")
SIZES = (4, 4, 2, 4, 4)
DEVICES = 512
HALF = 256
f32, bf16 = jnp.float32, jnp.bfloat16
VMEM = pl.BlockSpec(memory_space=pltpu.VMEM)
SMEM = pl.BlockSpec(memory_space=pltpu.SMEM)
ANY = pl.BlockSpec(memory_space=pl.ANY)
HBM = pl.BlockSpec(memory_space=pltpu.HBM)
PARAMS = pltpu.CompilerParams(vmem_limit_bytes=40 * 1024 * 1024)


def in_hbm(array):
    return pltpu.with_memory_space_constraint(array, pltpu.HBM)


def exchange(blocks, axes):
    return lax.all_to_all(blocks, axes, 0, 0, tiled=False)


def swap(block):
    return lax.ppermute(block, "core", [(0, 1), (1, 0)])


def along_y(block, step):
    return lax.ppermute(block, "y", [(y, (y + step) % 4) for y in range(4)])


def along_z(block, step):
    pairs = []
    for z in range(16):
        for x in range(4):
            for core in range(2):
                to = (z + step(x, core)) % 16
                pairs.append(
                    (((z // 4 * 4 + x) * 2 + core) * 4 + z % 4, ((to // 4 * 4 + x) * 2 + core) * 4 + to % 4)
                )
    return lax.ppermute(block, ("zh", "x", "core", "zl"), pairs)


def contract_rows(a, b):
    return lax.dot_general(a, b, (((0,), (0,)), ((), ())), preferred_element_type=f32)


def put_product(normed, grad, out, dtype):
    for part_at in range(8):
        y, first = part_at // 2, part_at % 2 * 2
        part = contract_rows(normed[:, part_at * HALF : (part_at + 1) * HALF], grad).astype(dtype)
        for x in range(4):
            for k in range(4):
                row = k // 2 * 128 + x * 32 + k % 2 * 16
                column = (first * 2 + k) * HALF
                out[y * 4 + x, :, column : column + HALF] = part[row : row + 16]


def norm_kernel(place, tokens_at, gain_at, grad_at, normed, inv_rms, theirs, tokens, norm_gain, key_grad, sem):
    quarters = [slice(i * 48, i * 48 + 48) for i in range(4)]
    copies = [(gain_at, norm_gain)] + [(tokens_at.at[rows], tokens.at[rows]) for rows in quarters]
    copies = [
        pltpu.make_async_copy(source, target, sem.at[i])
        for i, (source, target) in enumerate(copies + [(grad_at, key_grad)])
    ]
    for copy in copies:
        copy.start()
    copies[0].wait()
    for copy, rows in zip(copies[1:], quarters):
        copy.wait()
        wide = tokens[rows, :].astype(f32)
        inv = lax.rsqrt(jnp.mean(wide * wide, axis=1, keepdims=True) + eps)
        inv_rms[rows, :] = jnp.broadcast_to(inv, (48, 128))
        normed[rows, :] = (wide * inv * norm_gain[...]).astype(bf16)
    copies[5].wait()
    start = pl.multiple_of((1 - place[0]) * HALF, HALF)
    put_product(normed, key_grad[:, pl.ds(start, HALF)], theirs, bf16)


def mine_kernel(place, normed, key_grad, mine):
    start = pl.multiple_of(place[0] * HALF, HALF)
    put_product(normed, key_grad[:, pl.ds(start, HALF)], mine, f32)


def copy_out(pairs, sem):
    copies = [pltpu.make_async_copy(source, target, sem.at[i]) for i, (source, target) in enumerate(pairs)]
    for copy in copies:
        copy.start()
    return copies


def pair_kernel(mine, got, out, held, sem):
    copies = []
    for part in range(4):
        peers = slice(part * 4, part * 4 + 4)
        for peer in range(part * 4, part * 4 + 4):
            held[peer] = (mine[peer] + got[peer].astype(f32)).astype(bf16)
        copies += copy_out([(held.at[peers], out.at[peers])], sem.at[pl.ds(part, 1)])
    for copy in copies:
        copy.wait()


def two_rows(value):
    high = value.astype(bf16).astype(f32)
    row = lax.broadcasted_iota(jnp.int32, (8, 128), 0)
    return jnp.where(row == 0, high, jnp.where(row == 1, value - high, 0.0)).astype(bf16)


def square_kernel(place, square, shard, above, across, below, out, shards, products, held, sem):
    x, zl = place[1], place[3]
    for k in range(8):
        cols = slice(k * HALF, (k + 1) * HALF)
        total = square[0, :, cols].astype(f32)
        for sender in range(1, 16):
            total += square[sender, :, cols].astype(f32)
        shards[k // 2, k % 2 * 16 : k % 2 * 16 + 16] = total
    for j, piece in enumerate((shard, above, across, below)):
        which = lax.rem(zl + j, 4)
        rows = piece[pl.ds(pl.multiple_of(x * 32, 32), 32), :].astype(f32)
        products[which] = shards[which] * rows
    gain = lax.dot_general(
        jnp.ones((8, HALF), f32),
        products[...].reshape(128, HALF),
        (((1,), (1,)), ((), ())),
        preferred_element_type=f32,
        precision=lax.Precision.HIGHEST,
    )
    gains = two_rows(gain)
    for target in range(4):
        for k in range(4):
            held[target, :, k * HALF : (k + 1) * HALF] = shards[target, k * 8 : k * 8 + 8].astype(bf16)
        held[target, :, 4 * HALF :] = gains
    for copy in copy_out([(held, out.at[zh * 4 : zh * 4 + 4]) for zh in range(4)], sem):
        copy.wait()


def line_kernel(line, out, held, sem):
    total = line[0].astype(f32)
    for sender in range(1, 16):
        total += line[sender].astype(f32)
    gains = two_rows(jnp.broadcast_to(total[0:1, 4 * HALF :] + total[1:2, 4 * HALF :], (8, 128)))
    rows = total[:, : 4 * HALF].astype(bf16)
    for peer in range(8):
        held[peer, :, : 4 * HALF] = rows
        held[peer, :, 4 * HALF :] = gains
    for copy in copy_out([(held, out.at[y * 8 : y * 8 + 8]) for y in range(4)], sem):
        copy.wait()


def last_kernel(place, blocks, norm_gain, weight_grad, gain_grad):
    y = place[2]
    for x in range(4):
        for core in range(2):
            block = blocks[y * 8 + x * 2 + core].astype(f32) / DEVICES
            for k in range(4):
                at = x * 32 + k * 8
                weight_grad[at : at + 8, core * HALF : (core + 1) * HALF] = block[:, k * HALF : (k + 1) * HALF]
    rows_of = []
    for peer in range(16):
        gains = blocks[peer * 2, :, 4 * HALF :].astype(f32) + blocks[peer * 2 + 1, :, 4 * HALF :].astype(f32)
        rows_of.append(gains[0:1] + gains[1:2])
    sums = jnp.concatenate(rows_of, axis=0)
    lane = lax.broadcasted_iota(jnp.int32, (16, 128), 1)
    peer = lax.broadcasted_iota(jnp.int32, (16, 128), 0)
    spread = (
        lax.broadcasted_iota(jnp.int32, (128, 128), 0) % 32
        == lax.broadcasted_iota(jnp.int32, (128, 128), 1) % 32
    ).astype(f32)
    stacked = jnp.concatenate([jnp.where(lane // 32 == zl, sums, 0.0) for zl in range(4)], axis=0)
    moved = lax.dot_general(
        stacked, spread, (((1,), (0,)), ((), ())), preferred_element_type=f32,
        precision=lax.Precision.HIGHEST,
    )
    for row in range(4):
        for zl in range(4):
            picked = jnp.where(peer == row * 4 + lane // 32, moved[zl * 16 : zl * 16 + 16], 0.0)
            at = row * 4 + zl
            gain_grad[at : at + 1, :] = jnp.sum(picked, axis=0, keepdims=True) / (
                norm_gain[at : at + 1, :] * DEVICES
            )


def token_kernel(place, tokens, inv_rms, norm_gain, key_grad, *rest):
    pieces, (keys, tokens_grad, weight, sem) = rest[:4], rest[4:]
    core, y, zl = place[0], place[2], place[3]
    copies = []
    for step in range(4):
        for side in range(2):
            column = core * HALF if side == 0 else (1 - core) * HALF
            for j in range(4):
                row = (lax.rem(y + step, 4) * 4 + lax.rem(zl + j, 4)) * 128
                copies.append(
                    pltpu.make_async_copy(
                        pieces[side * 2 + step // 2].at[step % 2 * 4 + j],
                        weight.at[pl.ds(pl.multiple_of(row, 128), 128), pl.ds(pl.multiple_of(column, HALF), HALF)],
                        sem.at[len(copies)],
                    )
                )
    for copy in copies:
        copy.start()
    for copy in copies:
        copy.wait()
    for rows in (slice(0, 96), slice(96, 192)):
        inv = inv_rms[rows, 0:1]
        unit = tokens[rows, :].astype(f32) * inv
        normed = (unit * norm_gain[...]).astype(bf16)
        keys[rows, :] = jnp.dot(normed, weight[...], preferred_element_type=f32).astype(bf16)
        scaled = norm_gain[...] * lax.dot_general(
            key_grad[rows, :], weight[...], (((1,), (1,)), ((), ())), preferred_element_type=f32
        )
        mean = jnp.mean(scaled * unit, axis=1, keepdims=True)
        tokens_grad[rows, :] = (inv * (scaled - unit * mean)).astype(bf16)


def call(kernel, outs, ins, args, scratch=(), flops=0, out_specs=None):
    moved = sum(a.size * a.dtype.itemsize for a in args)
    return pl.pallas_call(
        kernel,
        out_shape=[jax.ShapeDtypeStruct(s, d) for s, d in outs],
        in_specs=ins,
        out_specs=out_specs or [VMEM] * len(outs),
        scratch_shapes=list(scratch),
        compiler_params=PARAMS,
        cost_estimate=pl.CostEstimate(flops=flops, bytes_accessed=2 * moved, transcendentals=0),
    )(*args)


def local(tokens, norm_gain, weight_codes, block_scales, key_grad):
    core = lax.axis_index("core")
    place = jnp.stack(
        [core, lax.axis_index("x"), lax.axis_index("y"), lax.axis_index("zl")]
    ).astype(jnp.int32)
    gain_row = norm_gain.reshape(1, 2048)

    codes = lax.dynamic_slice_in_dim(weight_codes, core * HALF, HALF, 1)
    scales = lax.dynamic_slice_in_dim(block_scales, core * HALF, HALF, 1)
    shard = (codes.astype(f32) * scales).astype(bf16)
    normed, inv_rms, theirs = call(
        norm_kernel,
        [((192, 2048), bf16), ((192, 128), f32), ((16, 16, 2048), bf16)],
        [SMEM, HBM, HBM, HBM],
        (place, in_hbm(tokens), in_hbm(gain_row), in_hbm(key_grad)),
        scratch=[
            pltpu.VMEM((192, 2048), bf16),
            pltpu.VMEM((1, 2048), f32),
            pltpu.VMEM((192, 512), bf16),
            pltpu.SemaphoreType.DMA((6,)),
        ],
        flops=2 * 192 * 2048 * 256,
    )
    got = swap(theirs)
    (mine,) = call(
        mine_kernel,
        [((16, 16, 2048), f32)],
        [SMEM, VMEM, VMEM],
        (place, normed, key_grad),
        flops=2 * 192 * 2048 * 256,
    )
    (pair,) = call(pair_kernel, [((16, 16, 2048), bf16)], [VMEM] * 2, (mine, got), scratch=[pltpu.VMEM((16, 16, 2048), bf16), pltpu.SemaphoreType.DMA((4,))], out_specs=[ANY])
    square = exchange(pair, ("y", "x"))

    shard_late, _ = lax.optimization_barrier((shard, pair))
    above = along_z(shard_late, lambda x, core: -1)
    across = along_z(shard_late, lambda x, core: (2, -2)[core])
    below = along_z(shard_late, lambda x, core: 1)
    stack = jnp.stack([shard, above, across, below])

    (payload,) = call(
        square_kernel,
        [((16, 8, 1152), bf16)],
        [SMEM] + [VMEM] * 5,
        (place, square, shard, above, across, below),
        scratch=[
            pltpu.VMEM((4, 32, HALF), f32),
            pltpu.VMEM((4, 32, HALF), f32),
            pltpu.VMEM((4, 8, 1152), bf16),
            pltpu.SemaphoreType.DMA((4,)),
        ],
        out_specs=[ANY],
    )
    line = exchange(payload, ("zh", "zl"))
    stack_late, _ = lax.optimization_barrier((stack, payload))
    one, two, three = (along_y(stack_late, -step) for step in (1, 2, 3))
    near = jnp.concatenate([stack, one], axis=0)
    line, near, three = lax.optimization_barrier((line, near, three))
    (blocks,) = call(
        line_kernel,
        [((32, 8, 1152), bf16)],
        [VMEM],
        (line,),
        scratch=[pltpu.VMEM((8, 8, 1152), bf16), pltpu.SemaphoreType.DMA((4,))],
        out_specs=[ANY],
    )
    near_late, two, _ = lax.optimization_barrier((near, two, blocks))
    far = jnp.concatenate([two, three], axis=0)
    pieces = (near, far, swap(near_late), swap(far))
    blocks = exchange(blocks, ("y", "x", "core"))
    keys, tokens_grad = call(
        token_kernel,
        [((192, 512), bf16), ((192, 2048), bf16)],
        [SMEM, VMEM, VMEM, VMEM, VMEM] + [ANY] * 4,
        (place, tokens, inv_rms, gain_row, key_grad, *pieces),
        scratch=[pltpu.VMEM((2048, 512), bf16), pltpu.SemaphoreType.DMA((32,))],
    )
    blocks, keys, tokens_grad = lax.optimization_barrier((blocks, keys, tokens_grad))
    weight_grad, gain_grad = call(
        last_kernel,
        [((128, 512), f32), ((16, 128), f32)],
        [SMEM, VMEM, VMEM],
        (place, blocks, norm_gain.reshape(16, 128)),
    )
    return keys, tokens_grad, weight_grad, gain_grad.reshape(2048)


def solution(mesh):
    fine = Mesh(mesh.devices.reshape(SIZES), AXES)
    everyone = P(AXES, None)
    group = P(("y", "zl"), None)
    in_specs = (everyone, P(), group, group, everyone)
    out_specs = (everyone, everyone, group, P())
    return jax.shard_map(local, mesh=fine, in_specs=in_specs, out_specs=out_specs, check_vma=False)
```

```python
import functools

import jax
import jax.numpy as jnp
from jax import lax
from jax.experimental import pallas as pl
from jax.experimental.pallas import tpu as pltpu
from jax.sharding import Mesh, PartitionSpec as P

eps = 1e-05
AXES = ("zh", "x", "core", "y", "zl")
SIZES = (4, 4, 2, 4, 4)
DEVICES = 512
HALF = 256
f32, bf16 = jnp.float32, jnp.bfloat16
VMEM = pl.BlockSpec(memory_space=pltpu.VMEM)
SMEM = pl.BlockSpec(memory_space=pltpu.SMEM)
ANY = pl.BlockSpec(memory_space=pl.ANY)
HBM = pl.BlockSpec(memory_space=pltpu.HBM)
PARAMS = pltpu.CompilerParams(vmem_limit_bytes=40 * 1024 * 1024)


def in_hbm(array):
    return pltpu.with_memory_space_constraint(array, pltpu.HBM)


def exchange(blocks, axes):
    return lax.all_to_all(blocks, axes, 0, 0, tiled=False)


def swap(block):
    return lax.ppermute(block, "core", [(0, 1), (1, 0)])


def along_y(block, step):
    return lax.ppermute(block, "y", [(y, (y + step) % 4) for y in range(4)])


def along_z(block, step):
    pairs = []
    for z in range(16):
        for x in range(4):
            for core in range(2):
                to = (z + step(x, core)) % 16
                pairs.append(
                    (((z // 4 * 4 + x) * 2 + core) * 4 + z % 4, ((to // 4 * 4 + x) * 2 + core) * 4 + to % 4)
                )
    return lax.ppermute(block, ("zh", "x", "core", "zl"), pairs)


def contract_rows(a, b):
    return lax.dot_general(a, b, (((0,), (0,)), ((), ())), preferred_element_type=f32)


def put_product(normed, grad, out, dtype):
    for part_at in range(8):
        y, first = part_at // 2, part_at % 2 * 2
        part = contract_rows(normed[:, part_at * HALF : (part_at + 1) * HALF], grad).astype(dtype)
        for x in range(4):
            for k in range(4):
                row = k // 2 * 128 + x * 32 + k % 2 * 16
                column = (first * 2 + k) * HALF
                out[y * 4 + x, :, column : column + HALF] = part[row : row + 16]


def norm_kernel(place, tokens_at, gain_at, grad_at, normed, inv_rms, theirs, tokens, norm_gain, key_grad, sem):
    quarters = [slice(i * 48, i * 48 + 48) for i in range(4)]
    copies = [(gain_at, norm_gain)] + [(tokens_at.at[rows], tokens.at[rows]) for rows in quarters]
    copies = [
        pltpu.make_async_copy(source, target, sem.at[i])
        for i, (source, target) in enumerate(copies + [(grad_at, key_grad)])
    ]
    for copy in copies:
        copy.start()
    copies[0].wait()
    for copy, rows in zip(copies[1:], quarters):
        copy.wait()
        wide = tokens[rows, :].astype(f32)
        inv = lax.rsqrt(jnp.mean(wide * wide, axis=1, keepdims=True) + eps)
        inv_rms[rows, :] = jnp.broadcast_to(inv, (48, 128))
        normed[rows, :] = (wide * inv * norm_gain[...]).astype(bf16)
    copies[5].wait()
    start = pl.multiple_of((1 - place[0]) * HALF, HALF)
    put_product(normed, key_grad[:, pl.ds(start, HALF)], theirs, bf16)


def mine_kernel(place, normed, key_grad, mine):
    start = pl.multiple_of(place[0] * HALF, HALF)
    put_product(normed, key_grad[:, pl.ds(start, HALF)], mine, f32)


def copy_out(pairs, sem):
    copies = [pltpu.make_async_copy(source, target, sem.at[i]) for i, (source, target) in enumerate(pairs)]
    for copy in copies:
        copy.start()
    return copies


def pair_kernel(mine, got, out, held, sem):
    copies = []
    for part in range(4):
        peers = slice(part * 4, part * 4 + 4)
        for peer in range(part * 4, part * 4 + 4):
            held[peer] = (mine[peer] + got[peer].astype(f32)).astype(bf16)
        copies += copy_out([(held.at[peers], out.at[peers])], sem.at[pl.ds(part, 1)])
    for copy in copies:
        copy.wait()


def two_rows(value):
    high = value.astype(bf16).astype(f32)
    row = lax.broadcasted_iota(jnp.int32, (8, 128), 0)
    return jnp.where(row == 0, high, jnp.where(row == 1, value - high, 0.0)).astype(bf16)


def square_kernel(place, square, shard, above, across, below, out, shards, products, held, sem):
    x, zl = place[1], place[3]
    for k in range(8):
        cols = slice(k * HALF, (k + 1) * HALF)
        total = square[0, :, cols].astype(f32)
        for sender in range(1, 16):
            total += square[sender, :, cols].astype(f32)
        shards[k // 2, k % 2 * 16 : k % 2 * 16 + 16] = total
    for j, piece in enumerate((shard, above, across, below)):
        which = lax.rem(zl + j, 4)
        rows = piece[pl.ds(pl.multiple_of(x * 32, 32), 32), :].astype(f32)
        products[which] = shards[which] * rows
    gain = lax.dot_general(
        jnp.ones((8, HALF), f32),
        products[...].reshape(128, HALF),
        (((1,), (1,)), ((), ())),
        preferred_element_type=f32,
        precision=lax.Precision.HIGHEST,
    )
    gains = two_rows(gain)
    for target in range(4):
        for k in range(4):
            held[target, :, k * HALF : (k + 1) * HALF] = shards[target, k * 8 : k * 8 + 8].astype(bf16)
        held[target, :, 4 * HALF :] = gains
    for copy in copy_out([(held, out.at[zh * 4 : zh * 4 + 4]) for zh in range(4)], sem):
        copy.wait()


def line_kernel(line, out, held, sem):
    total = line[0].astype(f32)
    for sender in range(1, 16):
        total += line[sender].astype(f32)
    gains = two_rows(jnp.broadcast_to(total[0:1, 4 * HALF :] + total[1:2, 4 * HALF :], (8, 128)))
    rows = total[:, : 4 * HALF].astype(bf16)
    for peer in range(8):
        held[peer, :, : 4 * HALF] = rows
        held[peer, :, 4 * HALF :] = gains
    for copy in copy_out([(held, out.at[y * 8 : y * 8 + 8]) for y in range(4)], sem):
        copy.wait()


def last_kernel(place, blocks, norm_gain, weight_grad, gain_grad):
    y = place[2]
    for x in range(4):
        for core in range(2):
            block = blocks[y * 8 + x * 2 + core].astype(f32) / DEVICES
            for k in range(4):
                at = x * 32 + k * 8
                weight_grad[at : at + 8, core * HALF : (core + 1) * HALF] = block[:, k * HALF : (k + 1) * HALF]
    rows_of = []
    for peer in range(16):
        gains = blocks[peer * 2, :, 4 * HALF :].astype(f32) + blocks[peer * 2 + 1, :, 4 * HALF :].astype(f32)
        rows_of.append(gains[0:1] + gains[1:2])
    sums = jnp.concatenate(rows_of, axis=0)
    lane = lax.broadcasted_iota(jnp.int32, (16, 128), 1)
    peer = lax.broadcasted_iota(jnp.int32, (16, 128), 0)
    spread = (
        lax.broadcasted_iota(jnp.int32, (128, 128), 0) % 32
        == lax.broadcasted_iota(jnp.int32, (128, 128), 1) % 32
    ).astype(f32)
    stacked = jnp.concatenate([jnp.where(lane // 32 == zl, sums, 0.0) for zl in range(4)], axis=0)
    moved = lax.dot_general(
        stacked, spread, (((1,), (0,)), ((), ())), preferred_element_type=f32,
        precision=lax.Precision.HIGHEST,
    )
    for row in range(4):
        for zl in range(4):
            picked = jnp.where(peer == row * 4 + lane // 32, moved[zl * 16 : zl * 16 + 16], 0.0)
            at = row * 4 + zl
            gain_grad[at : at + 1, :] = jnp.sum(picked, axis=0, keepdims=True) / (
                norm_gain[at : at + 1, :] * DEVICES
            )


def token_kernel(place, tokens, inv_rms, norm_gain, key_grad, *rest):
    pieces, (keys, tokens_grad, weight) = rest[:4], rest[4:]
    core, y, zl = place[0], place[2], place[3]
    for side in range(2):
        column = core * HALF if side == 0 else (1 - core) * HALF
        columns = pl.ds(pl.multiple_of(column, HALF), HALF)
        for step in range(4):
            for j in range(4):
                row = (lax.rem(y + step, 4) * 4 + lax.rem(zl + j, 4)) * 128
                weight[pl.ds(pl.multiple_of(row, 128), 128), columns] = pieces[side * 2 + step // 2][step % 2 * 4 + j]
    for rows in (slice(0, 96), slice(96, 192)):
        inv = inv_rms[rows, 0:1]
        unit = tokens[rows, :].astype(f32) * inv
        normed = (unit * norm_gain[...]).astype(bf16)
        keys[rows, :] = jnp.dot(normed, weight[...], preferred_element_type=f32).astype(bf16)
        scaled = norm_gain[...] * lax.dot_general(
            key_grad[rows, :], weight[...], (((1,), (1,)), ((), ())), preferred_element_type=f32
        )
        mean = jnp.mean(scaled * unit, axis=1, keepdims=True)
        tokens_grad[rows, :] = (inv * (scaled - unit * mean)).astype(bf16)


def call(kernel, outs, ins, args, scratch=(), flops=0, out_specs=None):
    moved = sum(a.size * a.dtype.itemsize for a in args)
    return pl.pallas_call(
        kernel,
        out_shape=[jax.ShapeDtypeStruct(s, d) for s, d in outs],
        in_specs=ins,
        out_specs=out_specs or [VMEM] * len(outs),
        scratch_shapes=list(scratch),
        compiler_params=PARAMS,
        cost_estimate=pl.CostEstimate(flops=flops, bytes_accessed=2 * moved, transcendentals=0),
    )(*args)


def local(tokens, norm_gain, weight_codes, block_scales, key_grad):
    core = lax.axis_index("core")
    place = jnp.stack(
        [core, lax.axis_index("x"), lax.axis_index("y"), lax.axis_index("zl")]
    ).astype(jnp.int32)
    gain_row = norm_gain.reshape(1, 2048)

    codes = lax.dynamic_slice_in_dim(weight_codes, core * HALF, HALF, 1)
    scales = lax.dynamic_slice_in_dim(block_scales, core * HALF, HALF, 1)
    shard = (codes.astype(f32) * scales).astype(bf16)
    normed, inv_rms, theirs = call(
        norm_kernel,
        [((192, 2048), bf16), ((192, 128), f32), ((16, 16, 2048), bf16)],
        [SMEM, HBM, HBM, HBM],
        (place, in_hbm(tokens), in_hbm(gain_row), in_hbm(key_grad)),
        scratch=[
            pltpu.VMEM((192, 2048), bf16),
            pltpu.VMEM((1, 2048), f32),
            pltpu.VMEM((192, 512), bf16),
            pltpu.SemaphoreType.DMA((6,)),
        ],
        flops=2 * 192 * 2048 * 256,
    )
    got = swap(theirs)
    (mine,) = call(
        mine_kernel,
        [((16, 16, 2048), f32)],
        [SMEM, VMEM, VMEM],
        (place, normed, key_grad),
        flops=2 * 192 * 2048 * 256,
    )
    (pair,) = call(pair_kernel, [((16, 16, 2048), bf16)], [VMEM] * 2, (mine, got), scratch=[pltpu.VMEM((16, 16, 2048), bf16), pltpu.SemaphoreType.DMA((4,))], out_specs=[ANY])
    square = exchange(pair, ("y", "x"))

    shard_late, _ = lax.optimization_barrier((shard, pair))
    above = along_z(shard_late, lambda x, core: -1)
    across = along_z(shard_late, lambda x, core: (2, -2)[core])
    below = along_z(shard_late, lambda x, core: 1)
    stack = jnp.stack([shard, above, across, below])

    (payload,) = call(
        square_kernel,
        [((16, 8, 1152), bf16)],
        [SMEM] + [VMEM] * 5,
        (place, square, shard, above, across, below),
        scratch=[
            pltpu.VMEM((4, 32, HALF), f32),
            pltpu.VMEM((4, 32, HALF), f32),
            pltpu.VMEM((4, 8, 1152), bf16),
            pltpu.SemaphoreType.DMA((4,)),
        ],
        out_specs=[ANY],
    )
    line = exchange(payload, ("zh", "zl"))
    stack_late, _ = lax.optimization_barrier((stack, payload))
    one, two, three = (along_y(stack_late, -step) for step in (1, 2, 3))
    near = jnp.concatenate([stack, one], axis=0)
    line, near = lax.optimization_barrier((line, near))
    (blocks,) = call(
        line_kernel,
        [((32, 8, 1152), bf16)],
        [VMEM],
        (line,),
        scratch=[pltpu.VMEM((8, 8, 1152), bf16), pltpu.SemaphoreType.DMA((4,))],
        out_specs=[ANY],
    )
    near_late, two, three, _ = lax.optimization_barrier((near, two, three, blocks))
    far = jnp.concatenate([two, three], axis=0)
    pieces = (near, far, swap(near_late), swap(far))
    blocks = exchange(blocks, ("y", "x", "core"))
    keys, tokens_grad = call(
        token_kernel,
        [((192, 512), bf16), ((192, 2048), bf16)],
        [SMEM] + [VMEM] * 8,
        (place, tokens, inv_rms, gain_row, key_grad, *pieces),
        scratch=[pltpu.VMEM((2048, 512), bf16)],
    )
    blocks, keys, tokens_grad = lax.optimization_barrier((blocks, keys, tokens_grad))
    weight_grad, gain_grad = call(
        last_kernel,
        [((128, 512), f32), ((16, 128), f32)],
        [SMEM, VMEM, VMEM],
        (place, blocks, norm_gain.reshape(16, 128)),
    )
    return keys, tokens_grad, weight_grad, gain_grad.reshape(2048)


def solution(mesh):
    fine = Mesh(mesh.devices.reshape(SIZES), AXES)
    everyone = P(AXES, None)
    group = P(("y", "zl"), None)
    in_specs = (everyone, P(), group, group, everyone)
    out_specs = (everyone, everyone, group, P())
    return jax.shard_map(local, mesh=fine, in_specs=in_specs, out_specs=out_specs, check_vma=False)
```

```python
import functools

import jax
import jax.numpy as jnp
from jax import lax
from jax.experimental import pallas as pl
from jax.experimental.pallas import tpu as pltpu
from jax.sharding import Mesh, PartitionSpec as P

eps = 1e-05
AXES = ("zh", "x", "core", "y", "zl")
SIZES = (4, 4, 2, 4, 4)
DEVICES = 512
HALF = 256
f32, bf16 = jnp.float32, jnp.bfloat16
VMEM = pl.BlockSpec(memory_space=pltpu.VMEM)
SMEM = pl.BlockSpec(memory_space=pltpu.SMEM)
ANY = pl.BlockSpec(memory_space=pl.ANY)
HBM = pl.BlockSpec(memory_space=pltpu.HBM)
PARAMS = pltpu.CompilerParams(vmem_limit_bytes=40 * 1024 * 1024)


def in_hbm(array):
    return pltpu.with_memory_space_constraint(array, pltpu.HBM)


def exchange(blocks, axes):
    return lax.all_to_all(blocks, axes, 0, 0, tiled=False)


def swap(block):
    return lax.ppermute(block, "core", [(0, 1), (1, 0)])


def along_y(block, step):
    return lax.ppermute(block, "y", [(y, (y + step) % 4) for y in range(4)])


def along_z(block, step):
    pairs = []
    for z in range(16):
        for x in range(4):
            for core in range(2):
                to = (z + step(x, core)) % 16
                pairs.append(
                    (((z // 4 * 4 + x) * 2 + core) * 4 + z % 4, ((to // 4 * 4 + x) * 2 + core) * 4 + to % 4)
                )
    return lax.ppermute(block, ("zh", "x", "core", "zl"), pairs)


def contract_rows(a, b):
    return lax.dot_general(a, b, (((0,), (0,)), ((), ())), preferred_element_type=f32)


def put_product(normed, grad, out, dtype):
    for part_at in range(8):
        y, first = part_at // 2, part_at % 2 * 2
        part = contract_rows(normed[:, part_at * HALF : (part_at + 1) * HALF], grad).astype(dtype)
        for x in range(4):
            for k in range(4):
                row = k // 2 * 128 + x * 32 + k % 2 * 16
                column = (first * 2 + k) * HALF
                out[y * 4 + x, :, column : column + HALF] = part[row : row + 16]


def norm_kernel(place, tokens_at, gain_at, grad_at, normed, inv_rms, theirs, tokens, norm_gain, key_grad, sem):
    quarters = [slice(i * 48, i * 48 + 48) for i in range(4)]
    copies = [(gain_at, norm_gain)] + [(tokens_at.at[rows], tokens.at[rows]) for rows in quarters]
    copies = [
        pltpu.make_async_copy(source, target, sem.at[i])
        for i, (source, target) in enumerate(copies + [(grad_at, key_grad)])
    ]
    for copy in copies:
        copy.start()
    copies[0].wait()
    for copy, rows in zip(copies[1:], quarters):
        copy.wait()
        wide = tokens[rows, :].astype(f32)
        inv = lax.rsqrt(jnp.mean(wide * wide, axis=1, keepdims=True) + eps)
        inv_rms[rows, :] = jnp.broadcast_to(inv, (48, 128))
        normed[rows, :] = (wide * inv * norm_gain[...]).astype(bf16)
    copies[5].wait()
    start = pl.multiple_of((1 - place[0]) * HALF, HALF)
    put_product(normed, key_grad[:, pl.ds(start, HALF)], theirs, bf16)


def mine_kernel(place, normed, key_grad, mine):
    start = pl.multiple_of(place[0] * HALF, HALF)
    put_product(normed, key_grad[:, pl.ds(start, HALF)], mine, f32)


def copy_out(pairs, sem):
    copies = [pltpu.make_async_copy(source, target, sem.at[i]) for i, (source, target) in enumerate(pairs)]
    for copy in copies:
        copy.start()
    return copies


def pair_kernel(mine, got, out, held, sem):
    copies = []
    for part in range(4):
        peers = slice(part * 4, part * 4 + 4)
        for peer in range(part * 4, part * 4 + 4):
            held[peer] = (mine[peer] + got[peer].astype(f32)).astype(bf16)
        copies += copy_out([(held.at[peers], out.at[peers])], sem.at[pl.ds(part, 1)])
    for copy in copies:
        copy.wait()


def two_rows(value):
    high = value.astype(bf16).astype(f32)
    row = lax.broadcasted_iota(jnp.int32, (8, 128), 0)
    return jnp.where(row == 0, high, jnp.where(row == 1, value - high, 0.0)).astype(bf16)


def square_kernel(place, square, shard, above, across, below, out, shards, products, held, sem):
    x, zl = place[1], place[3]
    for k in range(8):
        cols = slice(k * HALF, (k + 1) * HALF)
        total = square[0, :, cols].astype(f32)
        for sender in range(1, 16):
            total += square[sender, :, cols].astype(f32)
        shards[k // 2, k % 2 * 16 : k % 2 * 16 + 16] = total
    for j, piece in enumerate((shard, above, across, below)):
        which = lax.rem(zl + j, 4)
        rows = piece[pl.ds(pl.multiple_of(x * 32, 32), 32), :].astype(f32)
        products[which] = shards[which] * rows
    gain = lax.dot_general(
        jnp.ones((8, HALF), f32),
        products[...].reshape(128, HALF),
        (((1,), (1,)), ((), ())),
        preferred_element_type=f32,
        precision=lax.Precision.HIGHEST,
    )
    gains = two_rows(gain)
    for target in range(4):
        for k in range(4):
            held[target, :, k * HALF : (k + 1) * HALF] = shards[target, k * 8 : k * 8 + 8].astype(bf16)
        held[target, :, 4 * HALF :] = gains
    for copy in copy_out([(held.at[z // 4], out.at[z]) for z in range(16)], sem):
        copy.wait()


def line_kernel(line, out, held, sem):
    total = line[0].astype(f32)
    for sender in range(1, 16):
        total += line[sender].astype(f32)
    gains = two_rows(jnp.broadcast_to(total[0:1, 4 * HALF :] + total[1:2, 4 * HALF :], (8, 128)))
    rows = total[:, : 4 * HALF].astype(bf16)
    for peer in range(8):
        held[peer, :, : 4 * HALF] = rows
        held[peer, :, 4 * HALF :] = gains
    for copy in copy_out([(held, out.at[y * 8 : y * 8 + 8]) for y in range(4)], sem):
        copy.wait()


def last_kernel(place, blocks, norm_gain, weight_grad, gain_grad):
    y = place[2]
    for x in range(4):
        for core in range(2):
            block = blocks[x * 8 + core * 4 + y].astype(f32) / DEVICES
            for k in range(4):
                at = x * 32 + k * 8
                weight_grad[at : at + 8, core * HALF : (core + 1) * HALF] = block[:, k * HALF : (k + 1) * HALF]
    rows_of = []
    for peer in range(16):
        first = peer % 4 * 8 + peer // 4
        gains = blocks[first, :, 4 * HALF :].astype(f32) + blocks[first + 4, :, 4 * HALF :].astype(f32)
        rows_of.append(gains[0:1] + gains[1:2])
    sums = jnp.concatenate(rows_of, axis=0)
    lane = lax.broadcasted_iota(jnp.int32, (16, 128), 1)
    peer = lax.broadcasted_iota(jnp.int32, (16, 128), 0)
    spread = (
        lax.broadcasted_iota(jnp.int32, (128, 128), 0) % 32
        == lax.broadcasted_iota(jnp.int32, (128, 128), 1) % 32
    ).astype(f32)
    stacked = jnp.concatenate([jnp.where(lane // 32 == zl, sums, 0.0) for zl in range(4)], axis=0)
    moved = lax.dot_general(
        stacked, spread, (((1,), (0,)), ((), ())), preferred_element_type=f32,
        precision=lax.Precision.HIGHEST,
    )
    for row in range(4):
        for zl in range(4):
            picked = jnp.where(peer == row * 4 + lane // 32, moved[zl * 16 : zl * 16 + 16], 0.0)
            at = row * 4 + zl
            gain_grad[at : at + 1, :] = jnp.sum(picked, axis=0, keepdims=True) / (
                norm_gain[at : at + 1, :] * DEVICES
            )


def token_kernel(place, tokens, inv_rms, norm_gain, key_grad, *rest):
    pieces, (keys, tokens_grad, weight) = rest[:4], rest[4:]
    core, y, zl = place[0], place[2], place[3]
    for side in range(2):
        column = core * HALF if side == 0 else (1 - core) * HALF
        columns = pl.ds(pl.multiple_of(column, HALF), HALF)
        for step in range(4):
            for j in range(4):
                row = (lax.rem(y + step, 4) * 4 + lax.rem(zl + j, 4)) * 128
                weight[pl.ds(pl.multiple_of(row, 128), 128), columns] = pieces[side * 2 + step // 2][step % 2 * 4 + j]
    for rows in (slice(0, 96), slice(96, 192)):
        inv = inv_rms[rows, 0:1]
        unit = tokens[rows, :].astype(f32) * inv
        normed = (unit * norm_gain[...]).astype(bf16)
        keys[rows, :] = jnp.dot(normed, weight[...], preferred_element_type=f32).astype(bf16)
        scaled = norm_gain[...] * lax.dot_general(
            key_grad[rows, :], weight[...], (((1,), (1,)), ((), ())), preferred_element_type=f32
        )
        mean = jnp.mean(scaled * unit, axis=1, keepdims=True)
        tokens_grad[rows, :] = (inv * (scaled - unit * mean)).astype(bf16)


def call(kernel, outs, ins, args, scratch=(), flops=0, out_specs=None):
    moved = sum(a.size * a.dtype.itemsize for a in args)
    return pl.pallas_call(
        kernel,
        out_shape=[jax.ShapeDtypeStruct(s, d) for s, d in outs],
        in_specs=ins,
        out_specs=out_specs or [VMEM] * len(outs),
        scratch_shapes=list(scratch),
        compiler_params=PARAMS,
        cost_estimate=pl.CostEstimate(flops=flops, bytes_accessed=2 * moved, transcendentals=0),
    )(*args)


def local(tokens, norm_gain, weight_codes, block_scales, key_grad):
    core = lax.axis_index("core")
    place = jnp.stack(
        [core, lax.axis_index("x"), lax.axis_index("y"), lax.axis_index("zl")]
    ).astype(jnp.int32)
    gain_row = norm_gain.reshape(1, 2048)

    codes = lax.dynamic_slice_in_dim(weight_codes, core * HALF, HALF, 1)
    scales = lax.dynamic_slice_in_dim(block_scales, core * HALF, HALF, 1)
    shard = (codes.astype(f32) * scales).astype(bf16)
    normed, inv_rms, theirs = call(
        norm_kernel,
        [((192, 2048), bf16), ((192, 128), f32), ((16, 16, 2048), bf16)],
        [SMEM, HBM, HBM, HBM],
        (place, in_hbm(tokens), in_hbm(gain_row), in_hbm(key_grad)),
        scratch=[
            pltpu.VMEM((192, 2048), bf16),
            pltpu.VMEM((1, 2048), f32),
            pltpu.VMEM((192, 512), bf16),
            pltpu.SemaphoreType.DMA((6,)),
        ],
        flops=2 * 192 * 2048 * 256,
    )
    got = swap(theirs)
    (mine,) = call(
        mine_kernel,
        [((16, 16, 2048), f32)],
        [SMEM, VMEM, VMEM],
        (place, normed, key_grad),
        flops=2 * 192 * 2048 * 256,
    )
    (pair,) = call(pair_kernel, [((16, 16, 2048), bf16)], [VMEM] * 2, (mine, got), scratch=[pltpu.VMEM((16, 16, 2048), bf16), pltpu.SemaphoreType.DMA((4,))], out_specs=[ANY])
    square = exchange(pair, ("y", "x"))

    shard_late, _ = lax.optimization_barrier((shard, pair))
    above = along_z(shard_late, lambda x, core: -1)
    across = along_z(shard_late, lambda x, core: (2, -2)[core])
    below = along_z(shard_late, lambda x, core: 1)
    stack = jnp.stack([shard, above, across, below])

    (payload,) = call(
        square_kernel,
        [((16, 8, 1152), bf16)],
        [SMEM] + [VMEM] * 5,
        (place, square, shard, above, across, below),
        scratch=[
            pltpu.VMEM((4, 32, HALF), f32),
            pltpu.VMEM((4, 32, HALF), f32),
            pltpu.VMEM((4, 8, 1152), bf16),
            pltpu.SemaphoreType.DMA((16,)),
        ],
        out_specs=[ANY],
    )
    line = exchange(payload, ("zl", "zh"))
    stack_late, _ = lax.optimization_barrier((stack, payload))
    one, two, three = (along_y(stack_late, -step) for step in (1, 2, 3))
    near = jnp.concatenate([stack, one], axis=0)
    line, near = lax.optimization_barrier((line, near))
    (blocks,) = call(
        line_kernel,
        [((32, 8, 1152), bf16)],
        [VMEM],
        (line,),
        scratch=[pltpu.VMEM((8, 8, 1152), bf16), pltpu.SemaphoreType.DMA((4,))],
        out_specs=[ANY],
    )
    near_late, two, three, _ = lax.optimization_barrier((near, two, three, blocks))
    far = jnp.concatenate([two, three], axis=0)
    pieces = (near, far, swap(near_late), swap(far))
    blocks = exchange(blocks, ("x", "core", "y"))
    keys, tokens_grad = call(
        token_kernel,
        [((192, 512), bf16), ((192, 2048), bf16)],
        [SMEM] + [VMEM] * 8,
        (place, tokens, inv_rms, gain_row, key_grad, *pieces),
        scratch=[pltpu.VMEM((2048, 512), bf16)],
    )
    blocks, keys, tokens_grad = lax.optimization_barrier((blocks, keys, tokens_grad))
    weight_grad, gain_grad = call(
        last_kernel,
        [((128, 512), f32), ((16, 128), f32)],
        [SMEM, VMEM, VMEM],
        (place, blocks, norm_gain.reshape(16, 128)),
    )
    return keys, tokens_grad, weight_grad, gain_grad.reshape(2048)


def solution(mesh):
    fine = Mesh(mesh.devices.reshape(SIZES), AXES)
    everyone = P(AXES, None)
    group = P(("y", "zl"), None)
    in_specs = (everyone, P(), group, group, everyone)
    out_specs = (everyone, everyone, group, P())
    return jax.shard_map(local, mesh=fine, in_specs=in_specs, out_specs=out_specs, check_vma=False)
```

```python
import functools

import jax
import jax.numpy as jnp
from jax import lax
from jax.experimental import pallas as pl
from jax.experimental.pallas import tpu as pltpu
from jax.sharding import Mesh, PartitionSpec as P

eps = 1e-05
AXES = ("zh", "x", "core", "y", "zl")
SIZES = (4, 4, 2, 4, 4)
DEVICES = 512
HALF = 256
f32, bf16 = jnp.float32, jnp.bfloat16
VMEM = pl.BlockSpec(memory_space=pltpu.VMEM)
SMEM = pl.BlockSpec(memory_space=pltpu.SMEM)
ANY = pl.BlockSpec(memory_space=pl.ANY)
HBM = pl.BlockSpec(memory_space=pltpu.HBM)
PARAMS = pltpu.CompilerParams(vmem_limit_bytes=40 * 1024 * 1024)


def in_hbm(array):
    return pltpu.with_memory_space_constraint(array, pltpu.HBM)


def exchange(blocks, axes):
    return lax.all_to_all(blocks, axes, 0, 0, tiled=False)


def swap(block):
    return lax.ppermute(block, "core", [(0, 1), (1, 0)])


def along_y(block, step):
    return lax.ppermute(block, "y", [(y, (y + step) % 4) for y in range(4)])


def along_z(block, step):
    pairs = []
    for z in range(16):
        for x in range(4):
            for core in range(2):
                to = (z + step(x, core)) % 16
                pairs.append(
                    (((z // 4 * 4 + x) * 2 + core) * 4 + z % 4, ((to // 4 * 4 + x) * 2 + core) * 4 + to % 4)
                )
    return lax.ppermute(block, ("zh", "x", "core", "zl"), pairs)


def contract_rows(a, b):
    return lax.dot_general(a, b, (((0,), (0,)), ((), ())), preferred_element_type=f32)


def put_product(normed, grad, out, dtype):
    for part_at in range(8):
        y, first = part_at // 2, part_at % 2 * 2
        part = contract_rows(normed[:, part_at * HALF : (part_at + 1) * HALF], grad).astype(dtype)
        for x in range(4):
            for k in range(4):
                row = k // 2 * 128 + x * 32 + k % 2 * 16
                column = (first * 2 + k) * HALF
                out[y * 4 + x, :, column : column + HALF] = part[row : row + 16]


def norm_kernel(place, tokens_at, gain_at, grad_at, normed, inv_rms, theirs, tokens, norm_gain, key_grad, sem):
    quarters = [slice(i * 48, i * 48 + 48) for i in range(4)]
    copies = [(gain_at, norm_gain)] + [(tokens_at.at[rows], tokens.at[rows]) for rows in quarters]
    copies = [
        pltpu.make_async_copy(source, target, sem.at[i])
        for i, (source, target) in enumerate(copies + [(grad_at, key_grad)])
    ]
    for copy in copies:
        copy.start()
    copies[0].wait()
    for copy, rows in zip(copies[1:], quarters):
        copy.wait()
        wide = tokens[rows, :].astype(f32)
        inv = lax.rsqrt(jnp.mean(wide * wide, axis=1, keepdims=True) + eps)
        inv_rms[rows, :] = jnp.broadcast_to(inv, (48, 128))
        normed[rows, :] = (wide * inv * norm_gain[...]).astype(bf16)
    copies[5].wait()
    start = pl.multiple_of((1 - place[0]) * HALF, HALF)
    put_product(normed, key_grad[:, pl.ds(start, HALF)], theirs, bf16)


def mine_kernel(place, normed, key_grad, mine):
    start = pl.multiple_of(place[0] * HALF, HALF)
    put_product(normed, key_grad[:, pl.ds(start, HALF)], mine, f32)


def copy_out(pairs, sem):
    copies = [pltpu.make_async_copy(source, target, sem.at[i]) for i, (source, target) in enumerate(pairs)]
    for copy in copies:
        copy.start()
    return copies


def pair_kernel(mine, got, out, held, sem):
    copies = []
    for part in range(4):
        peers = slice(part * 4, part * 4 + 4)
        for peer in range(part * 4, part * 4 + 4):
            held[peer] = (mine[peer] + got[peer].astype(f32)).astype(bf16)
        copies += copy_out([(held.at[peers], out.at[peers])], sem.at[pl.ds(part, 1)])
    for copy in copies:
        copy.wait()


def two_rows(value):
    high = value.astype(bf16).astype(f32)
    row = lax.broadcasted_iota(jnp.int32, (8, 128), 0)
    return jnp.where(row == 0, high, jnp.where(row == 1, value - high, 0.0)).astype(bf16)


def square_kernel(place, square, shard, above, across, below, out, shards, products, held, sem):
    x, zl = place[1], place[3]
    for k in range(8):
        cols = slice(k * HALF, (k + 1) * HALF)
        total = square[0, :, cols].astype(f32)
        for sender in range(1, 16):
            total += square[sender, :, cols].astype(f32)
        shards[k // 2, k % 2 * 16 : k % 2 * 16 + 16] = total
    for j, piece in enumerate((shard, above, across, below)):
        which = lax.rem(zl + j, 4)
        rows = piece[pl.ds(pl.multiple_of(x * 32, 32), 32), :].astype(f32)
        products[which] = shards[which] * rows
    exact = products[...].reshape(128, HALF)
    high = exact.astype(bf16)
    low = (exact - high.astype(f32)).astype(bf16)
    ones = jnp.ones((8, HALF), bf16)
    gain = sum(
        lax.dot_general(ones, part, (((1,), (1,)), ((), ())), preferred_element_type=f32) for part in (high, low)
    )
    gains = two_rows(gain)
    for target in range(4):
        for k in range(4):
            held[target, :, k * HALF : (k + 1) * HALF] = shards[target, k * 8 : k * 8 + 8].astype(bf16)
        held[target, :, 4 * HALF :] = gains
    for copy in copy_out([(held, out.at[zh * 4 : zh * 4 + 4]) for zh in range(4)], sem):
        copy.wait()


def line_kernel(line, out, held, sem):
    total = line[0].astype(f32)
    for sender in range(1, 16):
        total += line[sender].astype(f32)
    gains = two_rows(jnp.broadcast_to(total[0:1, 4 * HALF :] + total[1:2, 4 * HALF :], (8, 128)))
    rows = total[:, : 4 * HALF].astype(bf16)
    for peer in range(8):
        held[peer, :, : 4 * HALF] = rows
        held[peer, :, 4 * HALF :] = gains
    for copy in copy_out([(held, out.at[y * 8 : y * 8 + 8]) for y in range(4)], sem):
        copy.wait()


def last_kernel(place, blocks, norm_gain, weight_grad, gain_grad, held, sem):
    y = place[2]
    copies = []
    for x in range(4):
        for core in range(2):
            block = blocks[y * 8 + x * 2 + core, :, : 4 * HALF].astype(f32) / DEVICES
            for k in range(4):
                at = x * 32 + k * 8
                held[at : at + 8, core * HALF : (core + 1) * HALF] = block[:, k * HALF : (k + 1) * HALF]
        rows = slice(x * 32, x * 32 + 32)
        copies += copy_out([(held.at[rows], weight_grad.at[rows])], sem.at[pl.ds(x, 1)])
    sums = blocks[:, :, 4 * HALF :].astype(f32).reshape(256, 128)
    lane = lax.broadcasted_iota(jnp.int32, (256, 128), 1) // 32
    own_x = lax.broadcasted_iota(jnp.int32, (64, 128), 0) // 16 == lax.broadcasted_iota(jnp.int32, (64, 128), 1) // 32
    spread = (
        lax.broadcasted_iota(jnp.int32, (128, 128), 0) % 32
        == lax.broadcasted_iota(jnp.int32, (128, 128), 1) % 32
    ).astype(f32).astype(bf16)
    for zl in range(4):
        moved = jnp.dot(
            jnp.where(lane == zl, sums, 0.0).astype(bf16), spread, preferred_element_type=f32
        )
        for row in range(4):
            picked = jnp.where(own_x, moved[row * 64 : row * 64 + 64], 0.0)
            at = row * 4 + zl
            gain_grad[at : at + 1, :] = jnp.sum(picked, axis=0, keepdims=True) / (
                norm_gain[at : at + 1, :] * DEVICES
            )
    for copy in copies:
        copy.wait()


def token_kernel(place, tokens, inv_rms, norm_gain, key_grad, *rest):
    pieces, (keys, tokens_grad, weight) = rest[:4], rest[4:]
    core, y, zl = place[0], place[2], place[3]
    for side in range(2):
        column = core * HALF if side == 0 else (1 - core) * HALF
        columns = pl.ds(pl.multiple_of(column, HALF), HALF)
        for step in range(4):
            for j in range(4):
                row = (lax.rem(y + step, 4) * 4 + lax.rem(zl + j, 4)) * 128
                weight[pl.ds(pl.multiple_of(row, 128), 128), columns] = pieces[side * 2 + step // 2][step % 2 * 4 + j]
    for rows in (slice(0, 96), slice(96, 192)):
        inv = inv_rms[rows, 0:1]
        unit = tokens[rows, :].astype(f32) * inv
        normed = (unit * norm_gain[...]).astype(bf16)
        keys[rows, :] = jnp.dot(normed, weight[...], preferred_element_type=f32).astype(bf16)
        scaled = norm_gain[...] * lax.dot_general(
            key_grad[rows, :], weight[...], (((1,), (1,)), ((), ())), preferred_element_type=f32
        )
        mean = jnp.mean(scaled * unit, axis=1, keepdims=True)
        tokens_grad[rows, :] = (inv * (scaled - unit * mean)).astype(bf16)


def call(kernel, outs, ins, args, scratch=(), flops=0, out_specs=None):
    moved = sum(a.size * a.dtype.itemsize for a in args)
    return pl.pallas_call(
        kernel,
        out_shape=[jax.ShapeDtypeStruct(s, d) for s, d in outs],
        in_specs=ins,
        out_specs=out_specs or [VMEM] * len(outs),
        scratch_shapes=list(scratch),
        compiler_params=PARAMS,
        cost_estimate=pl.CostEstimate(flops=flops, bytes_accessed=2 * moved, transcendentals=0),
    )(*args)


def local(tokens, norm_gain, weight_codes, block_scales, key_grad):
    core = lax.axis_index("core")
    place = jnp.stack(
        [core, lax.axis_index("x"), lax.axis_index("y"), lax.axis_index("zl")]
    ).astype(jnp.int32)
    gain_row = norm_gain.reshape(1, 2048)

    codes = lax.dynamic_slice_in_dim(weight_codes, core * HALF, HALF, 1)
    scales = lax.dynamic_slice_in_dim(block_scales, core * HALF, HALF, 1)
    shard = (codes.astype(f32) * scales).astype(bf16)
    normed, inv_rms, theirs = call(
        norm_kernel,
        [((192, 2048), bf16), ((192, 128), f32), ((16, 16, 2048), bf16)],
        [SMEM, HBM, HBM, HBM],
        (place, in_hbm(tokens), in_hbm(gain_row), in_hbm(key_grad)),
        scratch=[
            pltpu.VMEM((192, 2048), bf16),
            pltpu.VMEM((1, 2048), f32),
            pltpu.VMEM((192, 512), bf16),
            pltpu.SemaphoreType.DMA((6,)),
        ],
        flops=2 * 192 * 2048 * 256,
    )
    got = swap(theirs)
    (mine,) = call(
        mine_kernel,
        [((16, 16, 2048), f32)],
        [SMEM, VMEM, VMEM],
        (place, normed, key_grad),
        flops=2 * 192 * 2048 * 256,
    )
    (pair,) = call(pair_kernel, [((16, 16, 2048), bf16)], [VMEM] * 2, (mine, got), scratch=[pltpu.VMEM((16, 16, 2048), bf16), pltpu.SemaphoreType.DMA((4,))], out_specs=[ANY])
    square = exchange(pair, ("y", "x"))

    shard_late, _ = lax.optimization_barrier((shard, pair))
    above = along_z(shard_late, lambda x, core: -1)
    across = along_z(shard_late, lambda x, core: (2, -2)[core])
    below = along_z(shard_late, lambda x, core: 1)
    stack = jnp.stack([shard, above, across, below])

    (payload,) = call(
        square_kernel,
        [((16, 8, 1152), bf16)],
        [SMEM] + [VMEM] * 5,
        (place, square, shard, above, across, below),
        scratch=[
            pltpu.VMEM((4, 32, HALF), f32),
            pltpu.VMEM((4, 32, HALF), f32),
            pltpu.VMEM((4, 8, 1152), bf16),
            pltpu.SemaphoreType.DMA((4,)),
        ],
        out_specs=[ANY],
    )
    line = exchange(payload, ("zh", "zl"))
    stack_late, _ = lax.optimization_barrier((stack, payload))
    one, two, three = (along_y(stack_late, -step) for step in (1, 2, 3))
    near = jnp.concatenate([stack, one], axis=0)
    line, near = lax.optimization_barrier((line, near))
    (blocks,) = call(
        line_kernel,
        [((32, 8, 1152), bf16)],
        [VMEM],
        (line,),
        scratch=[pltpu.VMEM((8, 8, 1152), bf16), pltpu.SemaphoreType.DMA((4,))],
        out_specs=[ANY],
    )
    near_late, two, three, _ = lax.optimization_barrier((near, two, three, blocks))
    far = jnp.concatenate([two, three], axis=0)
    pieces = (near, far, swap(near_late), swap(far))
    blocks = exchange(blocks, ("y", "x", "core"))
    keys, tokens_grad = call(
        token_kernel,
        [((192, 512), bf16), ((192, 2048), bf16)],
        [SMEM] + [VMEM] * 8,
        (place, tokens, inv_rms, gain_row, key_grad, *pieces),
        scratch=[pltpu.VMEM((2048, 512), bf16)],
    )
    blocks, keys, tokens_grad = lax.optimization_barrier((blocks, keys, tokens_grad))
    weight_grad, gain_grad = call(
        last_kernel,
        [((128, 512), f32), ((16, 128), f32)],
        [SMEM, VMEM, VMEM],
        (place, blocks, norm_gain.reshape(16, 128)),
        scratch=[pltpu.VMEM((128, 512), f32), pltpu.SemaphoreType.DMA((4,))],
        out_specs=[ANY, VMEM],
    )
    return keys, tokens_grad, weight_grad, gain_grad.reshape(2048)


def solution(mesh):
    fine = Mesh(mesh.devices.reshape(SIZES), AXES)
    everyone = P(AXES, None)
    group = P(("y", "zl"), None)
    in_specs = (everyone, P(), group, group, everyone)
    out_specs = (everyone, everyone, group, P())
    return jax.shard_map(local, mesh=fine, in_specs=in_specs, out_specs=out_specs, check_vma=False)
```

```python
import functools

import jax
import jax.numpy as jnp
from jax import lax
from jax.experimental import pallas as pl
from jax.experimental.pallas import tpu as pltpu
from jax.sharding import Mesh, PartitionSpec as P

eps = 1e-05
AXES = ("zh", "x", "core", "y", "zl")
SIZES = (4, 4, 2, 4, 4)
DEVICES = 512
HALF = 256
f32, bf16 = jnp.float32, jnp.bfloat16
VMEM = pl.BlockSpec(memory_space=pltpu.VMEM)
SMEM = pl.BlockSpec(memory_space=pltpu.SMEM)
ANY = pl.BlockSpec(memory_space=pl.ANY)
HBM = pl.BlockSpec(memory_space=pltpu.HBM)
PARAMS = pltpu.CompilerParams(vmem_limit_bytes=40 * 1024 * 1024)


def in_hbm(array):
    return pltpu.with_memory_space_constraint(array, pltpu.HBM)


def exchange(blocks, axes):
    return lax.all_to_all(blocks, axes, 0, 0, tiled=False)


def swap(block):
    return lax.ppermute(block, "core", [(0, 1), (1, 0)])


def along_y(block, step):
    return lax.ppermute(block, "y", [(y, (y + step) % 4) for y in range(4)])


def along_z(block, step):
    pairs = []
    for z in range(16):
        for x in range(4):
            for core in range(2):
                to = (z + step(x, core)) % 16
                pairs.append(
                    (((z // 4 * 4 + x) * 2 + core) * 4 + z % 4, ((to // 4 * 4 + x) * 2 + core) * 4 + to % 4)
                )
    return lax.ppermute(block, ("zh", "x", "core", "zl"), pairs)


def contract_rows(a, b):
    return lax.dot_general(a, b, (((0,), (0,)), ((), ())), preferred_element_type=f32)


def put_product(normed, grad, out, dtype):
    for part_at in range(8):
        y, first = part_at // 2, part_at % 2 * 2
        part = contract_rows(normed[:, part_at * HALF : (part_at + 1) * HALF], grad).astype(dtype)
        for x in range(4):
            for k in range(4):
                row = k // 2 * 128 + x * 32 + k % 2 * 16
                column = (first * 2 + k) * HALF
                out[y * 4 + x, :, column : column + HALF] = part[row : row + 16]


def norm_kernel(place, tokens_at, gain_at, grad_at, normed, inv_rms, theirs, tokens, norm_gain, key_grad, sem):
    quarters = [slice(i * 48, i * 48 + 48) for i in range(4)]
    copies = [(gain_at, norm_gain)] + [(tokens_at.at[rows], tokens.at[rows]) for rows in quarters]
    copies = [
        pltpu.make_async_copy(source, target, sem.at[i])
        for i, (source, target) in enumerate(copies + [(grad_at, key_grad)])
    ]
    for copy in copies:
        copy.start()
    copies[0].wait()
    for copy, rows in zip(copies[1:], quarters):
        copy.wait()
        wide = tokens[rows, :].astype(f32)
        inv = lax.rsqrt(jnp.mean(wide * wide, axis=1, keepdims=True) + eps)
        inv_rms[rows, :] = jnp.broadcast_to(inv, (48, 128))
        normed[rows, :] = (wide * inv * norm_gain[...]).astype(bf16)
    copies[5].wait()
    start = pl.multiple_of((1 - place[0]) * HALF, HALF)
    put_product(normed, key_grad[:, pl.ds(start, HALF)], theirs, bf16)


def mine_kernel(place, normed, key_grad, mine):
    start = pl.multiple_of(place[0] * HALF, HALF)
    put_product(normed, key_grad[:, pl.ds(start, HALF)], mine, f32)


def copy_out(pairs, sem):
    copies = [pltpu.make_async_copy(source, target, sem.at[i]) for i, (source, target) in enumerate(pairs)]
    for copy in copies:
        copy.start()
    return copies


def pair_kernel(mine, got, out, held, sem):
    copies = []
    for part in range(4):
        peers = slice(part * 4, part * 4 + 4)
        for peer in range(part * 4, part * 4 + 4):
            held[peer] = (mine[peer] + got[peer].astype(f32)).astype(bf16)
        copies += copy_out([(held.at[peers], out.at[peers])], sem.at[pl.ds(part, 1)])
    for copy in copies:
        copy.wait()


def two_rows(value):
    high = value.astype(bf16).astype(f32)
    row = lax.broadcasted_iota(jnp.int32, (8, 128), 0)
    return jnp.where(row == 0, high, jnp.where(row == 1, value - high, 0.0)).astype(bf16)


def square_kernel(place, square, shard, above, across, below, out, shards, products, held, sem):
    x, zl = place[1], place[3]
    for k in range(8):
        cols = slice(k * HALF, (k + 1) * HALF)
        total = square[0, :, cols].astype(f32)
        for sender in range(1, 16):
            total += square[sender, :, cols].astype(f32)
        shards[k // 2, k % 2 * 16 : k % 2 * 16 + 16] = total
    for j, piece in enumerate((shard, above, across, below)):
        which = lax.rem(zl + j, 4)
        rows = piece[pl.ds(pl.multiple_of(x * 32, 32), 32), :].astype(f32)
        products[which] = shards[which] * rows
    exact = products[...].reshape(128, HALF)
    high = exact.astype(bf16)
    low = (exact - high.astype(f32)).astype(bf16)
    ones = jnp.ones((8, HALF), bf16)
    gain = sum(
        lax.dot_general(ones, part, (((1,), (1,)), ((), ())), preferred_element_type=f32) for part in (high, low)
    )
    gains = two_rows(gain)
    for target in range(4):
        for k in range(4):
            held[target, :, k * HALF : (k + 1) * HALF] = shards[target, k * 8 : k * 8 + 8].astype(bf16)
        held[target, :, 4 * HALF :] = gains
    for copy in copy_out([(held, out.at[zh * 4 : zh * 4 + 4]) for zh in range(4)], sem):
        copy.wait()


def line_kernel(line, out, held, sem):
    total = line[0].astype(f32)
    for sender in range(1, 16):
        total += line[sender].astype(f32)
    gains = two_rows(jnp.broadcast_to(total[0:1, 4 * HALF :] + total[1:2, 4 * HALF :], (8, 128)))
    rows = total[:, : 4 * HALF].astype(bf16)
    for peer in range(8):
        held[peer, :, : 4 * HALF] = rows
        held[peer, :, 4 * HALF :] = gains
    for copy in copy_out([(held, out.at[y * 8 : y * 8 + 8]) for y in range(4)], sem):
        copy.wait()


def last_kernel(place, blocks, norm_gain, weight_grad, gain_grad, held, sem):
    y = place[2]
    copies = []
    for x in range(4):
        for core in range(2):
            block = blocks[y * 8 + x * 2 + core, :, : 4 * HALF].astype(f32) / DEVICES
            for k in range(4):
                at = x * 32 + k * 8
                held[at : at + 8, core * HALF : (core + 1) * HALF] = block[:, k * HALF : (k + 1) * HALF]
        rows = slice(x * 32, x * 32 + 32)
        copies += copy_out([(held.at[rows], weight_grad.at[rows])], sem.at[pl.ds(x, 1)])
    rows_of = []
    for peer in range(16):
        gains = blocks[peer * 2, :, 4 * HALF :].astype(f32) + blocks[peer * 2 + 1, :, 4 * HALF :].astype(f32)
        rows_of.append(gains[0:1] + gains[1:2])
    sums = jnp.concatenate(rows_of, axis=0)
    lane = lax.broadcasted_iota(jnp.int32, (16, 128), 1)
    peer = lax.broadcasted_iota(jnp.int32, (16, 128), 0)
    spread = (
        lax.broadcasted_iota(jnp.int32, (128, 128), 0) % 32
        == lax.broadcasted_iota(jnp.int32, (128, 128), 1) % 32
    ).astype(f32)
    stacked = jnp.concatenate([jnp.where(lane // 32 == zl, sums, 0.0) for zl in range(4)], axis=0)
    moved = lax.dot_general(
        stacked, spread, (((1,), (0,)), ((), ())), preferred_element_type=f32,
        precision=lax.Precision.HIGHEST,
    )
    for row in range(4):
        for zl in range(4):
            picked = jnp.where(peer == row * 4 + lane // 32, moved[zl * 16 : zl * 16 + 16], 0.0)
            at = row * 4 + zl
            gain_grad[at : at + 1, :] = jnp.sum(picked, axis=0, keepdims=True) / (
                norm_gain[at : at + 1, :] * DEVICES
            )
    for copy in copies:
        copy.wait()


def token_kernel(place, tokens, inv_rms, norm_gain, key_grad, *rest):
    pieces, (keys, tokens_grad, weight) = rest[:4], rest[4:]
    core, y, zl = place[0], place[2], place[3]
    for side in range(2):
        column = core * HALF if side == 0 else (1 - core) * HALF
        columns = pl.ds(pl.multiple_of(column, HALF), HALF)
        for step in range(4):
            for j in range(4):
                row = (lax.rem(y + step, 4) * 4 + lax.rem(zl + j, 4)) * 128
                weight[pl.ds(pl.multiple_of(row, 128), 128), columns] = pieces[side * 2 + step // 2][step % 2 * 4 + j]
    for rows in (slice(0, 96), slice(96, 192)):
        inv = inv_rms[rows, 0:1]
        unit = tokens[rows, :].astype(f32) * inv
        normed = (unit * norm_gain[...]).astype(bf16)
        keys[rows, :] = jnp.dot(normed, weight[...], preferred_element_type=f32).astype(bf16)
        scaled = norm_gain[...] * lax.dot_general(
            key_grad[rows, :], weight[...], (((1,), (1,)), ((), ())), preferred_element_type=f32
        )
        mean = jnp.mean(scaled * unit, axis=1, keepdims=True)
        tokens_grad[rows, :] = (inv * (scaled - unit * mean)).astype(bf16)


def call(kernel, outs, ins, args, scratch=(), flops=0, out_specs=None):
    moved = sum(a.size * a.dtype.itemsize for a in args)
    return pl.pallas_call(
        kernel,
        out_shape=[jax.ShapeDtypeStruct(s, d) for s, d in outs],
        in_specs=ins,
        out_specs=out_specs or [VMEM] * len(outs),
        scratch_shapes=list(scratch),
        compiler_params=PARAMS,
        cost_estimate=pl.CostEstimate(flops=flops, bytes_accessed=2 * moved, transcendentals=0),
    )(*args)


def local(tokens, norm_gain, weight_codes, block_scales, key_grad):
    core = lax.axis_index("core")
    place = jnp.stack(
        [core, lax.axis_index("x"), lax.axis_index("y"), lax.axis_index("zl")]
    ).astype(jnp.int32)
    gain_row = norm_gain.reshape(1, 2048)

    codes = lax.dynamic_slice_in_dim(weight_codes, core * HALF, HALF, 1)
    scales = lax.dynamic_slice_in_dim(block_scales, core * HALF, HALF, 1)
    shard = (codes.astype(f32) * scales).astype(bf16)
    normed, inv_rms, theirs = call(
        norm_kernel,
        [((192, 2048), bf16), ((192, 128), f32), ((16, 16, 2048), bf16)],
        [SMEM, HBM, HBM, HBM],
        (place, in_hbm(tokens), in_hbm(gain_row), in_hbm(key_grad)),
        scratch=[
            pltpu.VMEM((192, 2048), bf16),
            pltpu.VMEM((1, 2048), f32),
            pltpu.VMEM((192, 512), bf16),
            pltpu.SemaphoreType.DMA((6,)),
        ],
        flops=2 * 192 * 2048 * 256,
    )
    got = swap(theirs)
    (mine,) = call(
        mine_kernel,
        [((16, 16, 2048), f32)],
        [SMEM, VMEM, VMEM],
        (place, normed, key_grad),
        flops=2 * 192 * 2048 * 256,
    )
    (pair,) = call(pair_kernel, [((16, 16, 2048), bf16)], [VMEM] * 2, (mine, got), scratch=[pltpu.VMEM((16, 16, 2048), bf16), pltpu.SemaphoreType.DMA((4,))], out_specs=[ANY])
    square = exchange(pair, ("y", "x"))

    shard_late, _ = lax.optimization_barrier((shard, pair))
    above = along_z(shard_late, lambda x, core: -1)
    across = along_z(shard_late, lambda x, core: (2, -2)[core])
    below = along_z(shard_late, lambda x, core: 1)
    stack = jnp.stack([shard, above, across, below])

    (payload,) = call(
        square_kernel,
        [((16, 8, 1152), bf16)],
        [SMEM] + [VMEM] * 5,
        (place, square, shard, above, across, below),
        scratch=[
            pltpu.VMEM((4, 32, HALF), f32),
            pltpu.VMEM((4, 32, HALF), f32),
            pltpu.VMEM((4, 8, 1152), bf16),
            pltpu.SemaphoreType.DMA((4,)),
        ],
        out_specs=[ANY],
    )
    line = exchange(payload, ("zh", "zl"))
    stack_late, _ = lax.optimization_barrier((stack, payload))
    one, two, three = (along_y(stack_late, -step) for step in (1, 2, 3))
    near = jnp.concatenate([stack, one], axis=0)
    line, near = lax.optimization_barrier((line, near))
    (blocks,) = call(
        line_kernel,
        [((32, 8, 1152), bf16)],
        [VMEM],
        (line,),
        scratch=[pltpu.VMEM((8, 8, 1152), bf16), pltpu.SemaphoreType.DMA((4,))],
        out_specs=[ANY],
    )
    near_late, two, three, _ = lax.optimization_barrier((near, two, three, blocks))
    far = jnp.concatenate([two, three], axis=0)
    pieces = (near, far, swap(near_late), swap(far))
    blocks = exchange(blocks, ("y", "x", "core"))
    keys, tokens_grad = call(
        token_kernel,
        [((192, 512), bf16), ((192, 2048), bf16)],
        [SMEM] + [VMEM] * 8,
        (place, tokens, inv_rms, gain_row, key_grad, *pieces),
        scratch=[pltpu.VMEM((2048, 512), bf16)],
    )
    blocks, keys, tokens_grad = lax.optimization_barrier((blocks, keys, tokens_grad))
    weight_grad, gain_grad = call(
        last_kernel,
        [((128, 512), f32), ((16, 128), f32)],
        [SMEM, VMEM, VMEM],
        (place, blocks, norm_gain.reshape(16, 128)),
        scratch=[pltpu.VMEM((128, 512), f32), pltpu.SemaphoreType.DMA((4,))],
        out_specs=[ANY, VMEM],
    )
    return keys, tokens_grad, weight_grad, gain_grad.reshape(2048)


def solution(mesh):
    fine = Mesh(mesh.devices.reshape(SIZES), AXES)
    everyone = P(AXES, None)
    group = P(("y", "zl"), None)
    in_specs = (everyone, P(), group, group, everyone)
    out_specs = (everyone, everyone, group, P())
    return jax.shard_map(local, mesh=fine, in_specs=in_specs, out_specs=out_specs, check_vma=False)
```
